512 devices in a mesh: ma: 32 (over z, core), row: 16 (over y, x).
Axes of the slice: x: 4, y: 4, z: 16, core: 2. Of those that a mesh axis runs over, the one named last changes fastest.
Arguments:
- seed_field: bfloat16 [4, 16, 2, 1024, 1024], P(None, 'row', None, 'ma'), may hold values from -6 to 6
- cotangent: bfloat16 [2, 16, 2, 1024, 1024], P(None, 'row', None, 'ma'), may hold values from -6 to 6
- step_size: float32 [1], replicated, may hold values from 0.25 to 1
- owner_list: int32 [1024], replicated, may hold values from 0 to 1023, as said below
Outputs:
- nonlinear: float32 [2, 16, 2, 1024, 1024], P(None, 'row', None, 'ma')
- seed_next: float32 [4, 16, 2, 1024, 1024], P(None, 'row', None, 'ma')
The draws below stay inside these ranges and needn't reach their ends.
Inputs may be any that keep to these rules, and one draw needn't show every extreme that they name: owner_list is a permutation of the wavenumbers; entries 32 d to 32 (d + 1) - 1 name the wavenumbers of owner d, and a block that holds m also holds 1023 - m.
All inputs are finite; a program needn't handle non-finite values.
Results may differ from the reference program's by a relative error of at most 0.0082.
Values may be sent and summed in bfloat16 or wider, within the bound.
A program may use at most 64 MiB of HBM per device.

```python
import math
import jax
import jax.numpy as jnp
from jax import lax

WAVES = 1024
DEGREES = 1024
NLAT = 1024
NLON = 2048
RADII = 16
OWN = 32


def draw_owner_list(key, part):
    pair_ids = jax.random.permutation(key, WAVES // 2).astype(jnp.int32).reshape(-1, OWN // 2)
    owner_rows = jnp.concatenate([pair_ids, WAVES - 1 - pair_ids], axis=1)
    return owner_rows.reshape(WAVES)


def block_scale(rng, shape, split, smallest, largest):
    level = 1.0
    for position, shards_of in split:
        steps = jax.random.uniform(jax.random.fold_in(jax.random.fold_in(rng, 6), position), (shards_of,), jnp.float32, smallest / len(split), largest / len(split))
        level = level * jnp.repeat(jnp.exp(steps), shape[position] // shards_of).reshape((-1,) + (1,) * (len(shape) - 1 - position))
    return level


def gaussian(rng, extent, spread, limit, pieces=(), kind=jnp.bfloat16):
    factor_of = block_scale(rng, extent, pieces, -0.22, 0.18) if pieces else 1.0
    values = jax.random.normal(rng, extent, jnp.float32) * spread * factor_of
    return jnp.minimum(jnp.maximum(values, -limit), limit).astype(kind)


def setup_inputs(seed: int = 0) -> dict:
    splits = jax.random.split(jax.random.key(seed), 5)
    return {
        "seed_field": gaussian(splits[0], (4, RADII, 2, DEGREES, WAVES), 1.0, 6.0, ((1, 16), (3, 32))),
        "cotangent": gaussian(splits[1], (2, RADII, 2, WAVES, DEGREES), 1.0, 6.0, ((1, 16), (3, 32))),
        "step_size": jnp.clip(jnp.exp(jax.random.uniform(splits[2], (1,), jnp.float32, math.log(0.25), math.log(1.0))), 0.25, 1.0),
        "owner_list": draw_owner_list(jax.random.fold_in(splits[4], 71), 0),
    }


def lat_cosines(theta_index):
    degree = jnp.arange(DEGREES, dtype=jnp.int32)
    phase_index = (2 * theta_index[:, None] + 1) * degree[None, :] % (4 * NLAT)
    return jnp.cos(phase_index.astype(jnp.float32) * (math.pi / (2 * NLAT))).astype(jnp.bfloat16)

def wave_cosines(wave_ids):
    points = jnp.arange(NLON, dtype=jnp.int32)
    phase_index = wave_ids[:, None] * points[None, :] % NLON
    angles = phase_index.astype(jnp.float32) * (2.0 * math.pi / NLON)
    return jnp.stack([jnp.cos(angles), -jnp.sin(angles)]).astype(jnp.bfloat16)

def radial_slope(values):
    zero_rim = jnp.zeros_like(values[:1])
    upper_side = jnp.concatenate([values[1:], zero_rim], axis=0)
    lower_side = jnp.concatenate([zero_rim, values[:-1]], axis=0)
    return 0.5 * (upper_side - lower_side)

def reference(seed_field, cotangent, step_size, owner_list):
    norm_scale = 2.0 / math.sqrt(DEGREES * WAVES)
    lat_wide = lat_cosines(jnp.arange(NLAT, dtype=jnp.int32)).astype(jnp.float32)
    wave_wide = wave_cosines(owner_list).astype(jnp.float32)
    live_mask = jnp.arange(DEGREES, dtype=jnp.int32)[None, :] >= owner_list[:, None]
    listed = jnp.swapaxes(jnp.take(seed_field, owner_list, axis=4), 3, 4)
    coeffs = jnp.where(live_mask, jnp.concatenate([listed, cotangent], axis=0), jnp.zeros((), jnp.bfloat16))

    def synthesize(radius_block):
        spec_rows = jnp.einsum('csml,tl->csmt', radius_block.astype(jnp.float32), lat_wide).astype(jnp.bfloat16)
        return norm_scale * jnp.einsum('csmt,smf->ctf', spec_rows.astype(jnp.float32), wave_wide)
    grid_field = lax.map(synthesize, jnp.swapaxes(coeffs, 0, 1))
    vel_tor = grid_field[:, 0]
    vel_pol = radial_slope(grid_field[:, 1])
    mag_tor = grid_field[:, 2]
    mag_pol = radial_slope(grid_field[:, 3])
    adj_vel = grid_field[:, 4]
    adj_mag = grid_field[:, 5]
    term_vel = mag_tor * mag_pol - vel_tor * vel_pol
    term_mag = vel_tor * mag_pol - vel_pol * mag_tor
    grad_vtor = -vel_pol * adj_vel + mag_pol * adj_mag
    grad_vpol = -vel_tor * adj_vel - mag_tor * adj_mag
    grad_mtor = mag_pol * adj_vel - vel_pol * adj_mag
    grad_mpol = mag_tor * adj_vel + vel_tor * adj_mag
    back_vpol = -radial_slope(grad_vpol)
    back_mpol = -radial_slope(grad_mpol)
    analysis_in = jnp.stack([term_vel, term_mag, grad_vtor, back_vpol, grad_mtor, back_mpol], axis=1).astype(jnp.bfloat16)
    live_wide = live_mask.astype(jnp.float32)

    def analyse(radius_block):
        back_rows = (norm_scale * jnp.einsum('ctf,smf->csmt', radius_block.astype(jnp.float32), wave_wide)).astype(jnp.bfloat16)
        return jnp.einsum('csmt,tl->csml', back_rows.astype(jnp.float32), lat_wide) * live_wide
    result = jnp.swapaxes(lax.map(analyse, analysis_in), 0, 1)
    nonlinear = result[:2]
    seed_next = listed.astype(jnp.float32) - step_size[0] * result[2:]
    return (nonlinear, seed_next)
```

```python
import functools
import math

import jax
import jax.numpy as jnp
import numpy as np
from jax import lax
from jax.experimental import pallas as pl
from jax.experimental.pallas import tpu as pltpu
from jax.sharding import PartitionSpec as P

MESH = pl.DeviceIdType.MESH
LANES = 128
OWN = 32
F32 = jnp.float32
BF16 = jnp.bfloat16

NT = (((1,), (1,)), ((), ()))
NN = (((1,), (0,)), ((), ()))


def lat_constant(size):
    phase = (2 * np.arange(size)[:, None] + 1) * np.arange(size)[None, :] % (4 * size)
    return np.cos(phase * (math.pi / (2 * size))).astype(jnp.bfloat16)


def wave_constant(waves, points):
    phase = np.arange(waves)[:, None] * np.arange(points)[None, :] % points
    angles = phase * (2.0 * math.pi / points)
    return np.stack([np.cos(angles), -np.sin(angles)]).astype(jnp.bfloat16)


def dot(a, b, dims):
    return lax.dot_general(a, b, dims, preferred_element_type=F32)


def kernel(
    na,
    nr,
    seed_ref,
    cot_ref,
    step_ref,
    owner_ref,
    lat_hbm,
    wave_hbm,
    non_ref,
    next_ref,
    lat,
    nat,
    table,
    onehot,
    owncol,
    mask,
    coef,
    listed,
    rows,
    grid,
    field,
    fwd_halo,
    back_send,
    back_halo,
    send,
    recv,
    load_sem,
    send_sem,
    recv_sem,
    halo_send_sem,
    halo_recv_sem,
):
    me = lax.axis_index("ma")
    radius = lax.axis_index("row")
    size = na * OWN
    points = 2 * size
    quads = na // 4
    chunk = min(256, size)
    wide = min(512, points)
    scale = 2.0 / size

    has_low = radius > 0
    has_high = radius < nr - 1
    barrier = pltpu.get_barrier_semaphore()

    def greet(step, carry):
        peer = lax.rem(me + step, na)
        pl.semaphore_signal(barrier, inc=1, device_id={"ma": peer}, device_id_type=MESH)
        return carry

    lax.fori_loop(1, na, greet, 0)

    @pl.when(has_low)
    def _():
        pl.semaphore_signal(barrier, inc=1, device_id={"row": radius - 1}, device_id_type=MESH)

    @pl.when(has_high)
    def _():
        pl.semaphore_signal(barrier, inc=1, device_id={"row": radius + 1}, device_id_type=MESH)

    load_wave = pltpu.make_async_copy(wave_hbm, nat, load_sem.at[0])
    load_lat = pltpu.make_async_copy(lat_hbm, lat, load_sem.at[1])
    load_wave.start()
    load_lat.start()

    def own_block(k):
        recv[k, me] = send[k, pl.ds(pl.multiple_of(me * OWN, OWN), OWN), :]

    def scatter(k):
        def one(step, carry):
            peer = lax.rem(me + step, na)
            pltpu.make_async_remote_copy(
                src_ref=send.at[k, pl.ds(pl.multiple_of(peer * OWN, OWN), OWN), :],
                dst_ref=recv.at[k, me],
                send_sem=send_sem.at[k],
                recv_sem=recv_sem.at[k],
                device_id={"ma": peer},
                device_id_type=MESH,
            ).start()
            return carry

        lax.fori_loop(1, na, one, 0)
        own_block(k)

    def arrived(k):
        part = recv.at[k, pl.ds(0, na - 1)]
        pltpu.make_async_copy(part, part, recv_sem.at[k]).wait()

    def sent(k):
        part = send.at[k, pl.ds(0, (na - 1) * OWN), :]
        pltpu.make_async_copy(part, part, send_sem.at[k]).wait()

    def halo_copies(src, dst, base):
        down = pltpu.make_async_remote_copy(
            src_ref=src,
            dst_ref=dst.at[1],
            send_sem=halo_send_sem.at[base],
            recv_sem=halo_recv_sem.at[base + 1],
            device_id={"row": jnp.maximum(radius - 1, 0)},
            device_id_type=MESH,
        )
        up = pltpu.make_async_remote_copy(
            src_ref=src,
            dst_ref=dst.at[0],
            send_sem=halo_send_sem.at[base + 1],
            recv_sem=halo_recv_sem.at[base],
            device_id={"row": jnp.minimum(radius + 1, nr - 1)},
            device_id_type=MESH,
        )
        return down, up

    def halo_start(src, dst, base):
        down, up = halo_copies(src, dst, base)

        @pl.when(has_low)
        def _():
            down.start()

        @pl.when(has_high)
        def _():
            up.start()

        @pl.when(jnp.logical_not(has_low))
        def _():
            dst[0] = jnp.zeros_like(dst[0])

        @pl.when(jnp.logical_not(has_high))
        def _():
            dst[1] = jnp.zeros_like(dst[1])

    def halo_wait(src, dst, base):
        down, up = halo_copies(src, dst, base)

        @pl.when(has_low)
        def _():
            up.wait_recv()

        @pl.when(has_high)
        def _():
            down.wait_recv()

    def halo_sent(src, dst, base):
        down, up = halo_copies(src, dst, base)

        @pl.when(has_low)
        def _():
            down.wait_send()

        @pl.when(has_high)
        def _():
            up.wait_send()

    group = lax.broadcasted_iota(jnp.int32, (OWN, LANES), 1) // OWN
    odd = lax.rem(group, 2) == 1
    high = group >= 2

    def regroup(k, put):
        def one(q, carry):
            x = [recv[k, 4 * q + a].astype(F32) for a in range(4)]
            y = [None] * 4
            for a in (0, 2):
                y[a] = jnp.where(odd, pltpu.roll(x[a + 1], 32, 1), x[a])
                y[a + 1] = jnp.where(odd, x[a + 1], pltpu.roll(x[a], 96, 1))
            z = [None] * 4
            for a in (0, 1):
                z[a] = jnp.where(high, pltpu.roll(y[a + 2], 64, 1), y[a])
                z[a + 2] = jnp.where(high, y[a + 2], pltpu.roll(y[a], 64, 1))
            columns = pl.ds(pl.multiple_of(q * LANES, LANES), LANES)
            for g in range(4):
                put(g, columns, z[g])
            return carry

        lax.fori_loop(0, quads, one, 0)

    def stacked(k, left):
        def one(i, carry):
            at = pl.ds(pl.multiple_of(i * chunk, chunk), chunk)
            send[k, at, :] = dot(left[at, :], coef[...], NT).astype(BF16)
            return carry

        lax.fori_loop(0, size // chunk, one, 0)

    def spread(b, carry):
        at = pl.ds(pl.multiple_of(b * LANES, LANES), LANES)
        column = jnp.transpose(jnp.broadcast_to(owner_ref[0:1, at], (LANES, LANES)))
        owncol[at, :] = column
        lane = lax.broadcasted_iota(jnp.int32, (LANES, LANES), 1)
        for c in range(size // LANES):
            onehot[at, c * LANES : (c + 1) * LANES] = jnp.where(
                column == lane + c * LANES, 1.0, 0.0
            ).astype(BF16)
        return carry

    lax.fori_loop(0, size // LANES, spread, 0)

    for k, first in ((0, 0), (1, 1)):
        for c in range(2):
            for s in range(2):
                g = 2 * c + s
                coef[g * OWN : (g + 1) * OWN, :] = seed_ref[first + 2 * c, s]
        stacked(k, onehot)
        if k == 0:
            pl.semaphore_wait(
                barrier, na - 1 + has_low.astype(jnp.int32) + has_high.astype(jnp.int32)
            )
        scatter(k)

    mine = owncol[pl.ds(pl.multiple_of(me * OWN, OWN), OWN), :]
    for c in range(size // LANES):
        lane = lax.broadcasted_iota(jnp.int32, (OWN, LANES), 1) + c * LANES
        mask[:, c * LANES : (c + 1) * LANES] = jnp.where(lane >= mine, 1.0, 0.0)

    load_lat.wait()
    for c in range(2):
        for s in range(2):
            g = 2 * c + s
            coef[g * OWN : (g + 1) * OWN, :] = jnp.where(
                mask[...] > 0.0, cot_ref[c, s].astype(F32), 0.0
            ).astype(BF16)
    stacked(4, lat)

    load_wave.wait()
    wide_steps = points // wide
    tall_steps = size // chunk

    def permute(i, carry):
        s = i // (wide_steps * tall_steps)
        rest = lax.rem(i, wide_steps * tall_steps)
        columns = pl.ds(pl.multiple_of(lax.rem(rest, wide_steps) * wide, wide), wide)
        top = pl.multiple_of((rest // wide_steps) * chunk, chunk)
        table[s, pl.ds(top, chunk), columns] = dot(
            onehot[pl.ds(top, chunk), :], nat[s, :, columns], NN
        ).astype(BF16)
        return carry

    lax.fori_loop(0, 2 * wide_steps * tall_steps, permute, 0)

    arrived(0)

    def keep_toroidal(g, columns, tile):
        listed[2 * (g // 2), g % 2, :, columns] = tile.astype(BF16)
        coef[g * OWN : (g + 1) * OWN, columns] = jnp.where(
            mask[:, columns] > 0.0, tile, 0.0
        ).astype(BF16)

    regroup(0, keep_toroidal)
    stacked(2, lat)
    scatter(2)

    arrived(1)

    def keep_poloidal(g, columns, tile):
        listed[2 * (g // 2) + 1, g % 2, :, columns] = tile.astype(BF16)
        rows[g * OWN : (g + 1) * OWN, columns] = tile.astype(BF16)

    regroup(1, keep_poloidal)
    halo_start(rows, fwd_halo, 0)
    halo_wait(rows, fwd_halo, 0)
    for g in range(4):
        at = slice(g * OWN, (g + 1) * OWN)
        slope = 0.5 * (fwd_halo[1, at, :].astype(F32) - fwd_halo[0, at, :].astype(F32))
        coef[at, :] = jnp.where(mask[...] > 0.0, slope, 0.0).astype(BF16)
    stacked(3, lat)
    scatter(3)
    scatter(4)

    def into_grid(base):
        def put(g, columns, tile):
            grid[base + g // 2, g % 2, :, columns] = tile.astype(BF16)

        return put

    arrived(2)
    regroup(2, into_grid(0))
    arrived(3)
    regroup(3, into_grid(2))

    def on_grid(first, count, columns):
        left = grid[first : first + count]
        total = None
        for s in range(2):
            part = dot(
                left[:, s].reshape(count * OWN, size), table[s, :, columns], NN
            )
            total = part if total is None else total + part
        total = total * scale
        return [total[c * OWN : (c + 1) * OWN] for c in range(count)]

    def terms(i, carry):
        columns = pl.ds(pl.multiple_of(i * wide, wide), wide)
        vel_tor, mag_tor, vel_pol, mag_pol = on_grid(0, 4, columns)
        for c, value in enumerate((vel_tor, mag_tor, vel_pol, mag_pol)):
            field[c, :, columns] = value
        back_send[0:OWN, columns] = (mag_tor * mag_pol - vel_tor * vel_pol).astype(BF16)
        back_send[OWN : 2 * OWN, columns] = (vel_tor * mag_pol - vel_pol * mag_tor).astype(BF16)
        return carry

    def analyse(k, source):
        def one(i, carry):
            at = pl.ds(pl.multiple_of(i * chunk, chunk), chunk)
            parts = [dot(table[s, at, :], source[...], NT) for s in range(2)]
            send[k, at, :] = (scale * jnp.concatenate(parts, axis=1)).astype(BF16)
            return carry

        lax.fori_loop(0, size // chunk, one, 0)

    lax.fori_loop(0, points // wide, terms, 0)
    analyse(5, back_send)
    scatter(5)

    arrived(4)
    regroup(4, into_grid(4))
    tor_grad = back_halo.at[2]

    def grads(i, carry):
        columns = pl.ds(pl.multiple_of(i * wide, wide), wide)
        adj_vel, adj_mag = on_grid(4, 2, columns)
        vel_tor, mag_tor, vel_pol, mag_pol = (field[c, :, columns] for c in range(4))
        back_send[0:OWN, columns] = (-vel_tor * adj_vel - mag_tor * adj_mag).astype(BF16)
        back_send[OWN : 2 * OWN, columns] = (mag_tor * adj_vel + vel_tor * adj_mag).astype(BF16)
        tor_grad[0:OWN, columns] = (-vel_pol * adj_vel + mag_pol * adj_mag).astype(BF16)
        tor_grad[OWN : 2 * OWN, columns] = (mag_pol * adj_vel - vel_pol * adj_mag).astype(BF16)
        return carry

    lax.fori_loop(0, points // wide, grads, 0)
    halo_start(back_send, back_halo, 2)
    analyse(6, tor_grad)
    scatter(6)
    halo_wait(back_send, back_halo, 2)
    tor_grad[...] = (
        0.5 * (back_halo[0].astype(F32) - back_halo[1].astype(F32))
    ).astype(BF16)
    analyse(7, tor_grad)
    scatter(7)

    step = step_ref[0]

    def finish(k, put):
        arrived(k)

        def keep(g, columns, tile):
            rows[g * OWN : (g + 1) * OWN, columns] = tile.astype(BF16)

        if k == 5:
            halo_sent(rows, fwd_halo, 0)
        regroup(k, keep)

        def one(i, carry):
            columns = pl.ds(pl.multiple_of(i * chunk, chunk), chunk)
            result = dot(rows[...], lat[:, columns], NN)
            live = mask[:, columns] > 0.0
            for g in range(4):
                put(
                    g // 2,
                    g % 2,
                    columns,
                    jnp.where(live, result[g * OWN : (g + 1) * OWN], 0.0),
                )
            return carry

        lax.fori_loop(0, size // chunk, one, 0)

    def put_term(s, c, columns, value):
        non_ref[c, s, :, columns] = value

    def put_seed(first):
        def put(s, c, columns, value):
            channel = 2 * c + first
            next_ref[channel, s, :, columns] = (
                listed[channel, s, :, columns].astype(F32) - step * value
            )

        return put

    finish(5, put_term)
    finish(6, put_seed(0))
    finish(7, put_seed(1))
    halo_sent(back_send, back_halo, 2)
    for k in range(8):
        sent(k)


def local(lat_table, wave_table, seed_field, cotangent, step_size, owner_list):
    na = lax.axis_size("ma")
    nr = lax.axis_size("row")
    size = na * OWN
    points = 2 * size
    vmem = pl.BlockSpec(memory_space=pltpu.VMEM)
    hbm = pl.BlockSpec(memory_space=pl.ANY)
    nonlinear, seed_next = pl.pallas_call(
        functools.partial(kernel, na, nr),
        out_shape=(
            jax.ShapeDtypeStruct((2, 2, OWN, size), F32),
            jax.ShapeDtypeStruct((4, 2, OWN, size), F32),
        ),
        in_specs=[vmem, vmem, pl.BlockSpec(memory_space=pltpu.SMEM), vmem, hbm, hbm],
        out_specs=(vmem, vmem),
        scratch_shapes=[
            pltpu.VMEM((size, size), BF16),
            pltpu.VMEM((2, size, points), BF16),
            pltpu.VMEM((2, size, points), BF16),
            pltpu.VMEM((size, size), BF16),
            pltpu.VMEM((size, LANES), jnp.int32),
            pltpu.VMEM((OWN, size), F32),
            pltpu.VMEM((4 * OWN, size), BF16),
            pltpu.VMEM((4, 2, OWN, size), BF16),
            pltpu.VMEM((4 * OWN, size), BF16),
            pltpu.VMEM((6, 2, OWN, size), BF16),
            pltpu.VMEM((4, OWN, points), F32),
            pltpu.VMEM((2, 4 * OWN, size), BF16),
            pltpu.VMEM((2 * OWN, points), BF16),
            pltpu.VMEM((3, 2 * OWN, points), BF16),
            pltpu.VMEM((8, size, LANES), BF16),
            pltpu.VMEM((8, na, OWN, LANES), BF16),
            pltpu.SemaphoreType.DMA((2,)),
            pltpu.SemaphoreType.DMA((8,)),
            pltpu.SemaphoreType.DMA((8,)),
            pltpu.SemaphoreType.DMA((4,)),
            pltpu.SemaphoreType.DMA((4,)),
        ],
        compiler_params=pltpu.CompilerParams(
            collective_id=0, has_side_effects=True, vmem_limit_bytes=56 << 20
        ),
    )(
        seed_field.reshape(4, 2, OWN, size),
        cotangent.reshape(2, 2, OWN, size),
        step_size,
        owner_list.reshape(1, size),
        lat_table,
        wave_table,
    )
    return (
        nonlinear.reshape(2, 1, 2, OWN, size),
        seed_next.reshape(4, 1, 2, OWN, size),
    )


def solution(mesh):
    split = P(None, "row", None, "ma", None)
    size = mesh.shape["ma"] * OWN
    lat_table = lat_constant(size)
    wave_table = wave_constant(size, 2 * size)
    body = jax.shard_map(
        local,
        mesh=mesh,
        in_specs=(P(), P(), split, split, P(), P()),
        out_specs=(split, split),
        check_vma=False,
    )

    def run(seed_field, cotangent, step_size, owner_list):
        return body(
            jnp.asarray(lat_table), jnp.asarray(wave_table), seed_field, cotangent, step_size, owner_list
        )

    return run
```

```python
import functools
import math

import jax
import jax.numpy as jnp
import numpy as np
from jax import lax
from jax.experimental import pallas as pl
from jax.experimental.pallas import tpu as pltpu
from jax.sharding import PartitionSpec as P

MESH = pl.DeviceIdType.MESH
LANES = 128
OWN = 32
F32 = jnp.float32
BF16 = jnp.bfloat16

NT = (((1,), (1,)), ((), ()))
NN = (((1,), (0,)), ((), ()))


def lat_constant(size):
    phase = (2 * np.arange(size)[:, None] + 1) * np.arange(size)[None, :] % (4 * size)
    return np.cos(phase * (math.pi / (2 * size))).astype(jnp.bfloat16)


def wave_constant(waves, points):
    phase = np.arange(waves)[:, None] * np.arange(points)[None, :] % points
    angles = phase * (2.0 * math.pi / points)
    return np.stack([np.cos(angles), -np.sin(angles)]).astype(jnp.bfloat16)


def dot(a, b, dims):
    return lax.dot_general(a, b, dims, preferred_element_type=F32)


def kernel(
    na,
    nr,
    seed_hbm,
    cot_hbm,
    step_hbm,
    owner_hbm,
    lat_hbm,
    wave_hbm,
    non_hbm,
    next_hbm,
    seed_ref,
    cot_ref,
    step_ref,
    owner_ref,
    non_ref,
    next_ref,
    lat,
    nat,
    table,
    onehot,
    owncol,
    mask,
    coef,
    listed,
    rows,
    grid,
    field,
    fwd_halo,
    back_send,
    back_halo,
    send,
    recv,
    load_sem,
    store_sem,
    send_sem,
    recv_sem,
    halo_send_sem,
    halo_recv_sem,
):
    me = lax.axis_index("ma")
    radius = lax.axis_index("row")
    size = na * OWN
    points = 2 * size
    quads = na // 4
    chunk = min(256, size)
    tall = min(512, size)
    wide = min(1024, points)
    scale = 2.0 / size

    has_low = radius > 0
    has_high = radius < nr - 1
    barrier = pltpu.get_barrier_semaphore()

    loads = [
        pltpu.make_async_copy(src, dst, load_sem.at[i])
        for i, (src, dst) in enumerate(
            (
                (owner_hbm, owner_ref),
                (seed_hbm, seed_ref),
                (lat_hbm, lat),
                (cot_hbm, cot_ref),
                (step_hbm, step_ref),
                (wave_hbm, nat),
            )
        )
    ]
    load_owner, load_seed, load_lat, load_cot, load_step, load_wave = loads
    for load in loads:
        load.start()

    def greet(step, carry):
        peer = lax.rem(me + step, na)
        pl.semaphore_signal(barrier, inc=1, device_id={"ma": peer}, device_id_type=MESH)
        return carry

    lax.fori_loop(1, na, greet, 0)

    @pl.when(has_low)
    def _():
        pl.semaphore_signal(barrier, inc=1, device_id={"row": radius - 1}, device_id_type=MESH)

    @pl.when(has_high)
    def _():
        pl.semaphore_signal(barrier, inc=1, device_id={"row": radius + 1}, device_id_type=MESH)

    def scatter(k, first, count):
        def one(i, carry):
            peer = first + i
            block = send.at[k, pl.ds(pl.multiple_of(peer * OWN, OWN), OWN), :]

            @pl.when(peer != me)
            def _():
                pltpu.make_async_remote_copy(
                    src_ref=block,
                    dst_ref=recv.at[k, me],
                    send_sem=send_sem.at[k],
                    recv_sem=recv_sem.at[k],
                    device_id={"ma": peer},
                    device_id_type=MESH,
                ).start()

            @pl.when(peer == me)
            def _():
                recv[k, me] = block[...]

            return carry

        lax.fori_loop(0, count, one, 0)

    def in_turn(k, height, rows_of, go=True):
        count = size // height
        peers = height // OWN

        def one(i, carry):
            turn = lax.rem(me // peers + i, count)
            at = pl.ds(pl.multiple_of(turn * height, height), height)
            send[k, at, :] = rows_of(at).astype(BF16)
            if go:
                scatter(k, turn * peers, peers)
            return carry

        lax.fori_loop(0, count, one, 0)

    def arrived(k):
        part = recv.at[k, pl.ds(0, na - 1)]
        pltpu.make_async_copy(part, part, recv_sem.at[k]).wait()

    def sent(k):
        part = send.at[k, pl.ds(0, (na - 1) * OWN), :]
        pltpu.make_async_copy(part, part, send_sem.at[k]).wait()

    def halo_copies(src, dst, base):
        down = pltpu.make_async_remote_copy(
            src_ref=src,
            dst_ref=dst.at[1],
            send_sem=halo_send_sem.at[base],
            recv_sem=halo_recv_sem.at[base + 1],
            device_id={"row": jnp.maximum(radius - 1, 0)},
            device_id_type=MESH,
        )
        up = pltpu.make_async_remote_copy(
            src_ref=src,
            dst_ref=dst.at[0],
            send_sem=halo_send_sem.at[base + 1],
            recv_sem=halo_recv_sem.at[base],
            device_id={"row": jnp.minimum(radius + 1, nr - 1)},
            device_id_type=MESH,
        )
        return down, up

    def halo_start(src, dst, base):
        height = src.shape[0] // 4

        def piece(i, carry):
            at = pl.ds(pl.multiple_of(i * height, height), height)
            down, up = halo_copies(src.at[at], dst.at[:, at], base)

            @pl.when(has_low)
            def _():
                down.start()

            @pl.when(has_high)
            def _():
                up.start()

            return carry

        lax.fori_loop(0, 4, piece, 0)

        @pl.when(jnp.logical_not(has_low))
        def _():
            dst[0] = jnp.zeros_like(dst[0])

        @pl.when(jnp.logical_not(has_high))
        def _():
            dst[1] = jnp.zeros_like(dst[1])

    def halo_wait(src, dst, base):
        down, up = halo_copies(src, dst, base)

        @pl.when(has_low)
        def _():
            up.wait_recv()

        @pl.when(has_high)
        def _():
            down.wait_recv()

    def halo_sent(src, dst, base):
        down, up = halo_copies(src, dst, base)

        @pl.when(has_low)
        def _():
            down.wait_send()

        @pl.when(has_high)
        def _():
            up.wait_send()

    group = lax.broadcasted_iota(jnp.int32, (OWN, LANES), 1) // OWN
    odd = lax.rem(group, 2) == 1
    high = group >= 2

    def regroup(k, put):
        def one(q, carry):
            x = [recv[k, 4 * q + a].astype(F32) for a in range(4)]
            y = [None] * 4
            for a in (0, 2):
                y[a] = jnp.where(odd, pltpu.roll(x[a + 1], 32, 1), x[a])
                y[a + 1] = jnp.where(odd, x[a + 1], pltpu.roll(x[a], 96, 1))
            z = [None] * 4
            for a in (0, 1):
                z[a] = jnp.where(high, pltpu.roll(y[a + 2], 64, 1), y[a])
                z[a + 2] = jnp.where(high, y[a + 2], pltpu.roll(y[a], 64, 1))
            columns = pl.ds(pl.multiple_of(q * LANES, LANES), LANES)
            for g in range(4):
                put(g, columns, z[g])
            return carry

        lax.fori_loop(0, quads, one, 0, unroll=min(4, quads))

    def stacked(k, left, height, go=True):
        in_turn(k, height, lambda at: dot(left[at, :], coef[...], NT), go)

    load_owner.wait()

    def spread(b, carry):
        at = pl.ds(pl.multiple_of(b * LANES, LANES), LANES)
        column = jnp.transpose(jnp.broadcast_to(owner_ref[0:1, at], (LANES, LANES)))
        owncol[at, :] = column
        lane = lax.broadcasted_iota(jnp.int32, (LANES, LANES), 1)
        for c in range(size // LANES):
            onehot[at, c * LANES : (c + 1) * LANES] = jnp.where(
                column == lane + c * LANES, 1.0, 0.0
            ).astype(BF16)
        return carry

    lax.fori_loop(0, size // LANES, spread, 0)

    load_seed.wait()
    pl.semaphore_wait(barrier, na - 1 + has_low.astype(jnp.int32) + has_high.astype(jnp.int32))
    for k in range(2):
        for c in range(2):
            for s in range(2):
                g = 2 * c + s
                coef[g * OWN : (g + 1) * OWN, :] = seed_ref[k + 2 * c, s]
        stacked(k, onehot, chunk)

    mine = owncol[pl.ds(pl.multiple_of(me * OWN, OWN), OWN), :]
    for c in range(size // LANES):
        lane = lax.broadcasted_iota(jnp.int32, (OWN, LANES), 1) + c * LANES
        mask[:, c * LANES : (c + 1) * LANES] = jnp.where(lane >= mine, 1.0, 0.0)

    load_lat.wait()
    load_cot.wait()
    load_step.wait()
    for c in range(2):
        for s in range(2):
            g = 2 * c + s
            coef[g * OWN : (g + 1) * OWN, :] = jnp.where(
                mask[...] > 0.0, cot_ref[c, s].astype(F32), 0.0
            ).astype(BF16)
    stacked(4, lat, tall, go=False)

    load_wave.wait()
    part = min(512, points)
    wide_steps = points // part
    tall_steps = size // tall

    def permute(i, carry):
        s = i // (wide_steps * tall_steps)
        rest = lax.rem(i, wide_steps * tall_steps)
        columns = pl.ds(pl.multiple_of(lax.rem(rest, wide_steps) * part, part), part)
        top = pl.multiple_of((rest // wide_steps) * tall, tall)
        table[s, pl.ds(top, tall), columns] = dot(
            onehot[pl.ds(top, tall), :], nat[s, :, columns], NN
        ).astype(BF16)
        return carry

    lax.fori_loop(0, 2 * wide_steps * tall_steps, permute, 0)

    arrived(0)

    def keep_toroidal(g, columns, tile):
        listed[2 * (g // 2), g % 2, :, columns] = tile.astype(BF16)
        coef[g * OWN : (g + 1) * OWN, columns] = jnp.where(
            mask[:, columns] > 0.0, tile, 0.0
        ).astype(BF16)

    regroup(0, keep_toroidal)
    stacked(2, lat, chunk)

    arrived(1)

    def keep_poloidal(g, columns, tile):
        listed[2 * (g // 2) + 1, g % 2, :, columns] = tile.astype(BF16)
        rows[g * OWN : (g + 1) * OWN, columns] = tile.astype(BF16)

    regroup(1, keep_poloidal)
    halo_start(rows, fwd_halo, 0)
    halo_wait(rows, fwd_halo, 0)
    for g in range(4):
        at = slice(g * OWN, (g + 1) * OWN)
        slope = 0.5 * (fwd_halo[1, at, :].astype(F32) - fwd_halo[0, at, :].astype(F32))
        coef[at, :] = jnp.where(mask[...] > 0.0, slope, 0.0).astype(BF16)
    stacked(3, lat, chunk)
    scatter(4, 0, na)

    def into_grid(base):
        def put(g, columns, tile):
            grid[base + g // 2, g % 2, :, columns] = tile.astype(BF16)

        return put

    arrived(2)
    regroup(2, into_grid(0))
    arrived(3)
    regroup(3, into_grid(2))

    def on_grid(first, count, columns):
        left = grid[first : first + count]
        total = None
        for s in range(2):
            part = dot(
                left[:, s].reshape(count * OWN, size), table[s, :, columns], NN
            )
            total = part if total is None else total + part
        total = total * scale
        return [total[c * OWN : (c + 1) * OWN] for c in range(count)]

    def terms(i, carry):
        columns = pl.ds(pl.multiple_of(i * wide, wide), wide)
        vel_tor, mag_tor, vel_pol, mag_pol = on_grid(0, 4, columns)
        for c, value in enumerate((vel_tor, mag_tor, vel_pol, mag_pol)):
            field[c, :, columns] = value
        back_send[0:OWN, columns] = (mag_tor * mag_pol - vel_tor * vel_pol).astype(BF16)
        back_send[OWN : 2 * OWN, columns] = (vel_tor * mag_pol - vel_pol * mag_tor).astype(BF16)
        return carry

    def analyse(k, source):
        def made(at):
            parts = [dot(table[s, at, :], source[...], NT) for s in range(2)]
            return scale * jnp.concatenate(parts, axis=1)

        in_turn(k, tall, made)

    lax.fori_loop(0, points // wide, terms, 0)
    analyse(5, back_send)

    arrived(4)
    regroup(4, into_grid(4))
    tor_grad = back_halo.at[2]

    def grads(i, carry):
        columns = pl.ds(pl.multiple_of(i * wide, wide), wide)
        adj_vel, adj_mag = on_grid(4, 2, columns)
        vel_tor, mag_tor, vel_pol, mag_pol = (field[c, :, columns] for c in range(4))
        back_send[0:OWN, columns] = (-vel_tor * adj_vel - mag_tor * adj_mag).astype(BF16)
        back_send[OWN : 2 * OWN, columns] = (mag_tor * adj_vel + vel_tor * adj_mag).astype(BF16)
        tor_grad[0:OWN, columns] = (-vel_pol * adj_vel + mag_pol * adj_mag).astype(BF16)
        tor_grad[OWN : 2 * OWN, columns] = (mag_pol * adj_vel - vel_pol * adj_mag).astype(BF16)
        return carry

    lax.fori_loop(0, points // wide, grads, 0)
    halo_start(back_send, back_halo, 2)
    analyse(6, tor_grad)
    halo_wait(back_send, back_halo, 2)
    tor_grad[...] = (
        0.5 * (back_halo[0].astype(F32) - back_halo[1].astype(F32))
    ).astype(BF16)
    analyse(7, tor_grad)

    step = jnp.broadcast_to(step_ref[...].reshape(1, 1), (OWN, chunk))

    def finish(k, put):
        arrived(k)

        def keep(g, columns, tile):
            rows[g * OWN : (g + 1) * OWN, columns] = tile.astype(BF16)

        if k == 5:
            halo_sent(rows, fwd_halo, 0)
        regroup(k, keep)

        def one(i, carry):
            columns = pl.ds(pl.multiple_of(i * chunk, chunk), chunk)
            result = dot(rows[...], lat[:, columns], NN)
            live = mask[:, columns] > 0.0
            for g in range(4):
                put(
                    g // 2,
                    g % 2,
                    columns,
                    jnp.where(live, result[g * OWN : (g + 1) * OWN], 0.0),
                )
            return carry

        lax.fori_loop(0, size // chunk, one, 0)

    def put_term(s, c, columns, value):
        non_ref[c, s, :, columns] = value

    def put_seed(first):
        def put(s, c, columns, value):
            channel = 2 * c + first
            next_ref[channel, s, :, columns] = (
                listed[channel, s, :, columns].astype(F32) - step * value
            )

        return put

    stores = [pltpu.make_async_copy(non_ref, non_hbm, store_sem.at[0])]
    for channel in range(4):
        stores.append(
            pltpu.make_async_copy(
                next_ref.at[channel], next_hbm.at[channel], store_sem.at[channel + 1]
            )
        )
    finish(5, put_term)
    stores[0].start()
    finish(6, put_seed(0))
    stores[1].start()
    stores[3].start()
    finish(7, put_seed(1))
    stores[2].start()
    stores[4].start()
    halo_sent(back_send, back_halo, 2)
    for k in range(8):
        sent(k)
    for store in stores:
        store.wait()


def settle(non_in, next_in, non_out, next_out, sem):
    copies = [pltpu.make_async_copy(non_in, non_out, sem.at[0])]
    for channel in range(4):
        copies.append(
            pltpu.make_async_copy(next_in.at[channel], next_out.at[channel], sem.at[channel + 1])
        )
    for copy in copies:
        copy.start()
    for copy in copies:
        copy.wait()


def local(lat_table, wave_table, seed_field, cotangent, step_size, owner_list):
    na = lax.axis_size("ma")
    nr = lax.axis_size("row")
    size = na * OWN
    points = 2 * size
    hbm = pl.BlockSpec(memory_space=pl.ANY)
    shapes = (
        jax.ShapeDtypeStruct((2, 2, OWN, size), F32),
        jax.ShapeDtypeStruct((4, 2, OWN, size), F32),
    )
    outputs = pl.pallas_call(
        functools.partial(kernel, na, nr),
        out_shape=shapes,
        in_specs=[pl.BlockSpec(memory_space=pltpu.HBM)] * 6,
        out_specs=(hbm, hbm),
        scratch_shapes=[
            pltpu.VMEM((4, 2, OWN, size), BF16),
            pltpu.VMEM((2, 2, OWN, size), BF16),
            pltpu.VMEM((1,), F32),
            pltpu.VMEM((1, size), jnp.int32),
            pltpu.VMEM((2, 2, OWN, size), F32),
            pltpu.VMEM((4, 2, OWN, size), F32),
            pltpu.VMEM((size, size), BF16),
            pltpu.VMEM((2, size, points), BF16),
            pltpu.VMEM((2, size, points), BF16),
            pltpu.VMEM((size, size), BF16),
            pltpu.VMEM((size, LANES), jnp.int32),
            pltpu.VMEM((OWN, size), F32),
            pltpu.VMEM((4 * OWN, size), BF16),
            pltpu.VMEM((4, 2, OWN, size), BF16),
            pltpu.VMEM((4 * OWN, size), BF16),
            pltpu.VMEM((6, 2, OWN, size), BF16),
            pltpu.VMEM((4, OWN, points), F32),
            pltpu.VMEM((2, 4 * OWN, size), BF16),
            pltpu.VMEM((2 * OWN, points), BF16),
            pltpu.VMEM((3, 2 * OWN, points), BF16),
            pltpu.VMEM((8, size, LANES), BF16),
            pltpu.VMEM((8, na, OWN, LANES), BF16),
            pltpu.SemaphoreType.DMA((6,)),
            pltpu.SemaphoreType.DMA((5,)),
            pltpu.SemaphoreType.DMA((8,)),
            pltpu.SemaphoreType.DMA((8,)),
            pltpu.SemaphoreType.DMA((4,)),
            pltpu.SemaphoreType.DMA((4,)),
        ],
        compiler_params=pltpu.CompilerParams(
            collective_id=0, has_side_effects=True, vmem_limit_bytes=56 << 20
        ),
    )(
        seed_field.reshape(4, 2, OWN, size),
        cotangent.reshape(2, 2, OWN, size),
        step_size,
        owner_list.reshape(1, size),
        lat_table,
        wave_table,
    )
    nonlinear, seed_next = pl.pallas_call(
        settle,
        out_shape=shapes,
        in_specs=[hbm] * 2,
        out_specs=(hbm, hbm),
        scratch_shapes=[pltpu.SemaphoreType.DMA((5,))],
        compiler_params=pltpu.CompilerParams(vmem_limit_bytes=56 << 20),
    )(*outputs)
    return (
        nonlinear.reshape(2, 1, 2, OWN, size),
        seed_next.reshape(4, 1, 2, OWN, size),
    )


def solution(mesh):
    split = P(None, "row", None, "ma", None)
    size = mesh.shape["ma"] * OWN
    lat_table = lat_constant(size)
    wave_table = wave_constant(size, 2 * size)
    body = jax.shard_map(
        local,
        mesh=mesh,
        in_specs=(P(), P(), split, split, P(), P()),
        out_specs=(split, split),
        check_vma=False,
    )

    def run(seed_field, cotangent, step_size, owner_list):
        return body(
            jnp.asarray(lat_table), jnp.asarray(wave_table), seed_field, cotangent, step_size, owner_list
        )

    return run
```

```python
import functools
import math

import jax
import jax.numpy as jnp
import numpy as np
from jax import lax
from jax.experimental import pallas as pl
from jax.experimental.pallas import tpu as pltpu
from jax.sharding import PartitionSpec as P

MESH = pl.DeviceIdType.MESH
LANES = 128
OWN = 32
F32 = jnp.float32
BF16 = jnp.bfloat16

NT = (((1,), (1,)), ((), ()))
NN = (((1,), (0,)), ((), ()))


def lat_constant(size):
    phase = (2 * np.arange(size)[:, None] + 1) * np.arange(size)[None, :] % (4 * size)
    return np.cos(phase * (math.pi / (2 * size))).astype(jnp.bfloat16)


def wave_constant(waves, points):
    phase = np.arange(waves)[:, None] * np.arange(points)[None, :] % points
    angles = phase * (2.0 * math.pi / points)
    return np.stack([np.cos(angles), -np.sin(angles)]).astype(jnp.bfloat16)


def dot(a, b, dims):
    return lax.dot_general(a, b, dims, preferred_element_type=F32)


def kernel(
    na,
    nr,
    seed_hbm,
    cot_hbm,
    step_hbm,
    owner_hbm,
    lat_hbm,
    wave_hbm,
    non_ref,
    next_ref,
    seed_ref,
    cot_ref,
    step_ref,
    owner_ref,
    lat,
    nat,
    table,
    onehot,
    owncol,
    mask,
    coef,
    listed,
    rows,
    grid,
    field,
    fwd_halo,
    back_send,
    back_halo,
    send,
    recv,
    load_sem,
    send_sem,
    recv_sem,
    halo_send_sem,
    halo_recv_sem,
):
    me = lax.axis_index("ma")
    radius = lax.axis_index("row")
    size = na * OWN
    points = 2 * size
    quads = na // 4
    chunk = min(256, size)
    tall = min(512, size)
    wide = min(1024, points)
    scale = 2.0 / size

    has_low = radius > 0
    has_high = radius < nr - 1
    barrier = pltpu.get_barrier_semaphore()

    loads = [
        pltpu.make_async_copy(src, dst, load_sem.at[i])
        for i, (src, dst) in enumerate(
            (
                (owner_hbm, owner_ref),
                (seed_hbm, seed_ref),
                (lat_hbm, lat),
                (cot_hbm, cot_ref),
                (step_hbm, step_ref),
                (wave_hbm, nat),
            )
        )
    ]
    load_owner, load_seed, load_lat, load_cot, load_step, load_wave = loads
    for load in loads:
        load.start()

    def greet(step, carry):
        peer = lax.rem(me + step, na)
        pl.semaphore_signal(barrier, inc=1, device_id={"ma": peer}, device_id_type=MESH)
        return carry

    lax.fori_loop(1, na, greet, 0)

    @pl.when(has_low)
    def _():
        pl.semaphore_signal(barrier, inc=1, device_id={"row": radius - 1}, device_id_type=MESH)

    @pl.when(has_high)
    def _():
        pl.semaphore_signal(barrier, inc=1, device_id={"row": radius + 1}, device_id_type=MESH)

    def scatter(k, first, count):
        def one(i, carry):
            peer = first + i
            block = send.at[k, pl.ds(pl.multiple_of(peer * OWN, OWN), OWN), :]

            @pl.when(peer != me)
            def _():
                pltpu.make_async_remote_copy(
                    src_ref=block,
                    dst_ref=recv.at[k, me],
                    send_sem=send_sem.at[k],
                    recv_sem=recv_sem.at[k],
                    device_id={"ma": peer},
                    device_id_type=MESH,
                ).start()

            @pl.when(peer == me)
            def _():
                recv[k, me] = block[...]

            return carry

        lax.fori_loop(0, count, one, 0)

    def in_turn(k, height, rows_of, go=True):
        count = size // height
        peers = height // OWN

        def one(i, carry):
            turn = lax.rem(me // peers + i, count)
            at = pl.ds(pl.multiple_of(turn * height, height), height)
            send[k, at, :] = rows_of(at).astype(BF16)
            if go:
                scatter(k, turn * peers, peers)
            return carry

        lax.fori_loop(0, count, one, 0)

    def arrived(k):
        part = recv.at[k, pl.ds(0, na - 1)]
        pltpu.make_async_copy(part, part, recv_sem.at[k]).wait()

    def sent(k):
        part = send.at[k, pl.ds(0, (na - 1) * OWN), :]
        pltpu.make_async_copy(part, part, send_sem.at[k]).wait()

    def halo_copies(src, dst, base):
        down = pltpu.make_async_remote_copy(
            src_ref=src,
            dst_ref=dst.at[1],
            send_sem=halo_send_sem.at[base],
            recv_sem=halo_recv_sem.at[base + 1],
            device_id={"row": jnp.maximum(radius - 1, 0)},
            device_id_type=MESH,
        )
        up = pltpu.make_async_remote_copy(
            src_ref=src,
            dst_ref=dst.at[0],
            send_sem=halo_send_sem.at[base + 1],
            recv_sem=halo_recv_sem.at[base],
            device_id={"row": jnp.minimum(radius + 1, nr - 1)},
            device_id_type=MESH,
        )
        return down, up

    def halo_start(src, dst, base):
        height = src.shape[0] // 4

        def piece(i, carry):
            at = pl.ds(pl.multiple_of(i * height, height), height)
            down, up = halo_copies(src.at[at], dst.at[:, at], base)

            @pl.when(has_low)
            def _():
                down.start()

            @pl.when(has_high)
            def _():
                up.start()

            return carry

        lax.fori_loop(0, 4, piece, 0)

        @pl.when(jnp.logical_not(has_low))
        def _():
            dst[0] = jnp.zeros_like(dst[0])

        @pl.when(jnp.logical_not(has_high))
        def _():
            dst[1] = jnp.zeros_like(dst[1])

    def halo_wait(src, dst, base):
        down, up = halo_copies(src, dst, base)

        @pl.when(has_low)
        def _():
            up.wait_recv()

        @pl.when(has_high)
        def _():
            down.wait_recv()

    def halo_sent(src, dst, base):
        down, up = halo_copies(src, dst, base)

        @pl.when(has_low)
        def _():
            down.wait_send()

        @pl.when(has_high)
        def _():
            up.wait_send()

    group = lax.broadcasted_iota(jnp.int32, (OWN, LANES), 1) // OWN
    odd = lax.rem(group, 2) == 1
    high = group >= 2

    def regroup(k, put):
        def one(q, carry):
            x = [recv[k, 4 * q + a].astype(F32) for a in range(4)]
            y = [None] * 4
            for a in (0, 2):
                y[a] = jnp.where(odd, pltpu.roll(x[a + 1], 32, 1), x[a])
                y[a + 1] = jnp.where(odd, x[a + 1], pltpu.roll(x[a], 96, 1))
            z = [None] * 4
            for a in (0, 1):
                z[a] = jnp.where(high, pltpu.roll(y[a + 2], 64, 1), y[a])
                z[a + 2] = jnp.where(high, y[a + 2], pltpu.roll(y[a], 64, 1))
            columns = pl.ds(pl.multiple_of(q * LANES, LANES), LANES)
            for g in range(4):
                put(g, columns, z[g])
            return carry

        lax.fori_loop(0, quads, one, 0, unroll=min(4, quads))

    def stacked(k, left, height, go=True):
        in_turn(k, height, lambda at: dot(left[at, :], coef[...], NT), go)

    load_owner.wait()

    def spread(b, carry):
        at = pl.ds(pl.multiple_of(b * LANES, LANES), LANES)
        column = jnp.transpose(jnp.broadcast_to(owner_ref[0:1, at], (LANES, LANES)))
        owncol[at, :] = column
        lane = lax.broadcasted_iota(jnp.int32, (LANES, LANES), 1)
        for c in range(size // LANES):
            onehot[at, c * LANES : (c + 1) * LANES] = jnp.where(
                column == lane + c * LANES, 1.0, 0.0
            ).astype(BF16)
        return carry

    lax.fori_loop(0, size // LANES, spread, 0)

    load_seed.wait()
    pl.semaphore_wait(barrier, na - 1 + has_low.astype(jnp.int32) + has_high.astype(jnp.int32))
    for k in range(2):
        for c in range(2):
            for s in range(2):
                g = 2 * c + s
                coef[g * OWN : (g + 1) * OWN, :] = seed_ref[k + 2 * c, s]
        stacked(k, onehot, chunk)

    mine = owncol[pl.ds(pl.multiple_of(me * OWN, OWN), OWN), :]
    for c in range(size // LANES):
        lane = lax.broadcasted_iota(jnp.int32, (OWN, LANES), 1) + c * LANES
        mask[:, c * LANES : (c + 1) * LANES] = jnp.where(lane >= mine, 1.0, 0.0)

    load_lat.wait()
    load_cot.wait()
    load_step.wait()
    for c in range(2):
        for s in range(2):
            g = 2 * c + s
            coef[g * OWN : (g + 1) * OWN, :] = jnp.where(
                mask[...] > 0.0, cot_ref[c, s].astype(F32), 0.0
            ).astype(BF16)
    stacked(4, lat, tall, go=False)

    load_wave.wait()
    part = min(512, points)
    wide_steps = points // part
    tall_steps = size // tall

    def permute(i, carry):
        s = i // (wide_steps * tall_steps)
        rest = lax.rem(i, wide_steps * tall_steps)
        columns = pl.ds(pl.multiple_of(lax.rem(rest, wide_steps) * part, part), part)
        top = pl.multiple_of((rest // wide_steps) * tall, tall)
        table[s, pl.ds(top, tall), columns] = dot(
            onehot[pl.ds(top, tall), :], nat[s, :, columns], NN
        ).astype(BF16)
        return carry

    lax.fori_loop(0, 2 * wide_steps * tall_steps, permute, 0)

    arrived(0)

    def keep_toroidal(g, columns, tile):
        listed[2 * (g // 2), g % 2, :, columns] = tile.astype(BF16)
        coef[g * OWN : (g + 1) * OWN, columns] = jnp.where(
            mask[:, columns] > 0.0, tile, 0.0
        ).astype(BF16)

    regroup(0, keep_toroidal)
    stacked(2, lat, chunk)

    arrived(1)

    def keep_poloidal(g, columns, tile):
        listed[2 * (g // 2) + 1, g % 2, :, columns] = tile.astype(BF16)
        rows[g * OWN : (g + 1) * OWN, columns] = tile.astype(BF16)

    regroup(1, keep_poloidal)
    halo_start(rows, fwd_halo, 0)
    halo_wait(rows, fwd_halo, 0)
    for g in range(4):
        at = slice(g * OWN, (g + 1) * OWN)
        slope = 0.5 * (fwd_halo[1, at, :].astype(F32) - fwd_halo[0, at, :].astype(F32))
        coef[at, :] = jnp.where(mask[...] > 0.0, slope, 0.0).astype(BF16)
    stacked(3, lat, chunk)
    scatter(4, 0, na)

    def into_grid(base):
        def put(g, columns, tile):
            grid[base + g // 2, g % 2, :, columns] = tile.astype(BF16)

        return put

    arrived(2)
    regroup(2, into_grid(0))
    arrived(3)
    regroup(3, into_grid(2))

    def on_grid(first, count, columns):
        left = grid[first : first + count]
        total = None
        for s in range(2):
            part = dot(
                left[:, s].reshape(count * OWN, size), table[s, :, columns], NN
            )
            total = part if total is None else total + part
        total = total * scale
        return [total[c * OWN : (c + 1) * OWN] for c in range(count)]

    def terms(i, carry):
        columns = pl.ds(pl.multiple_of(i * wide, wide), wide)
        vel_tor, mag_tor, vel_pol, mag_pol = on_grid(0, 4, columns)
        for c, value in enumerate((vel_tor, mag_tor, vel_pol, mag_pol)):
            field[c, :, columns] = value
        back_send[0:OWN, columns] = (mag_tor * mag_pol - vel_tor * vel_pol).astype(BF16)
        back_send[OWN : 2 * OWN, columns] = (vel_tor * mag_pol - vel_pol * mag_tor).astype(BF16)
        return carry

    def analyse(k, source):
        def made(at):
            parts = [dot(table[s, at, :], source[...], NT) for s in range(2)]
            return scale * jnp.concatenate(parts, axis=1)

        in_turn(k, tall, made)

    lax.fori_loop(0, points // wide, terms, 0)
    analyse(5, back_send)

    arrived(4)
    regroup(4, into_grid(4))
    tor_grad = back_halo.at[2]

    def grads(i, carry):
        columns = pl.ds(pl.multiple_of(i * wide, wide), wide)
        adj_vel, adj_mag = on_grid(4, 2, columns)
        vel_tor, mag_tor, vel_pol, mag_pol = (field[c, :, columns] for c in range(4))
        back_send[0:OWN, columns] = (-vel_tor * adj_vel - mag_tor * adj_mag).astype(BF16)
        back_send[OWN : 2 * OWN, columns] = (mag_tor * adj_vel + vel_tor * adj_mag).astype(BF16)
        tor_grad[0:OWN, columns] = (-vel_pol * adj_vel + mag_pol * adj_mag).astype(BF16)
        tor_grad[OWN : 2 * OWN, columns] = (mag_pol * adj_vel - vel_pol * adj_mag).astype(BF16)
        return carry

    lax.fori_loop(0, points // wide, grads, 0)
    halo_start(back_send, back_halo, 2)
    analyse(6, tor_grad)
    halo_wait(back_send, back_halo, 2)
    tor_grad[...] = (
        0.5 * (back_halo[0].astype(F32) - back_halo[1].astype(F32))
    ).astype(BF16)
    analyse(7, tor_grad)

    step = jnp.broadcast_to(step_ref[...].reshape(1, 1), (OWN, chunk))

    def finish(k, put):
        arrived(k)

        def keep(g, columns, tile):
            rows[g * OWN : (g + 1) * OWN, columns] = tile.astype(BF16)

        if k == 5:
            halo_sent(rows, fwd_halo, 0)
        regroup(k, keep)

        def one(i, carry):
            columns = pl.ds(pl.multiple_of(i * chunk, chunk), chunk)
            result = dot(rows[...], lat[:, columns], NN)
            live = mask[:, columns] > 0.0
            for g in range(4):
                put(
                    g // 2,
                    g % 2,
                    columns,
                    jnp.where(live, result[g * OWN : (g + 1) * OWN], 0.0),
                )
            return carry

        lax.fori_loop(0, size // chunk, one, 0)

    def put_term(s, c, columns, value):
        non_ref[c, s, :, columns] = value

    def put_seed(first):
        def put(s, c, columns, value):
            channel = 2 * c + first
            next_ref[channel, s, :, columns] = (
                listed[channel, s, :, columns].astype(F32) - step * value
            )

        return put

    finish(5, put_term)
    finish(6, put_seed(0))
    finish(7, put_seed(1))
    halo_sent(back_send, back_halo, 2)
    for k in range(8):
        sent(k)


def settle(non_in, next_in, non_out, next_out, store_sem):
    stores = [pltpu.make_async_copy(non_in, non_out, store_sem.at[0])]
    for channel in range(4):
        stores.append(
            pltpu.make_async_copy(
                next_in.at[channel], next_out.at[channel], store_sem.at[channel + 1]
            )
        )
    for store in stores:
        store.start()
    for store in stores:
        store.wait()


def local(lat_table, wave_table, seed_field, cotangent, step_size, owner_list):
    na = lax.axis_size("ma")
    nr = lax.axis_size("row")
    size = na * OWN
    points = 2 * size
    hbm = pl.BlockSpec(memory_space=pl.ANY)
    shapes = (
        jax.ShapeDtypeStruct((2, 2, OWN, size), F32),
        jax.ShapeDtypeStruct((4, 2, OWN, size), F32),
    )
    outputs = pl.pallas_call(
        functools.partial(kernel, na, nr),
        out_shape=(pltpu.VMEM(shapes[0].shape, F32), pltpu.VMEM(shapes[1].shape, F32)),
        in_specs=[pl.BlockSpec(memory_space=pltpu.HBM)] * 6,
        out_specs=(pl.BlockSpec(memory_space=pltpu.VMEM),) * 2,
        scratch_shapes=[
            pltpu.VMEM((4, 2, OWN, size), BF16),
            pltpu.VMEM((2, 2, OWN, size), BF16),
            pltpu.VMEM((1,), F32),
            pltpu.VMEM((1, size), jnp.int32),
            pltpu.VMEM((size, size), BF16),
            pltpu.VMEM((2, size, points), BF16),
            pltpu.VMEM((2, size, points), BF16),
            pltpu.VMEM((size, size), BF16),
            pltpu.VMEM((size, LANES), jnp.int32),
            pltpu.VMEM((OWN, size), F32),
            pltpu.VMEM((4 * OWN, size), BF16),
            pltpu.VMEM((4, 2, OWN, size), BF16),
            pltpu.VMEM((4 * OWN, size), BF16),
            pltpu.VMEM((6, 2, OWN, size), BF16),
            pltpu.VMEM((4, OWN, points), F32),
            pltpu.VMEM((2, 4 * OWN, size), BF16),
            pltpu.VMEM((2 * OWN, points), BF16),
            pltpu.VMEM((3, 2 * OWN, points), BF16),
            pltpu.VMEM((8, size, LANES), BF16),
            pltpu.VMEM((8, na, OWN, LANES), BF16),
            pltpu.SemaphoreType.DMA((6,)),
            pltpu.SemaphoreType.DMA((8,)),
            pltpu.SemaphoreType.DMA((8,)),
            pltpu.SemaphoreType.DMA((4,)),
            pltpu.SemaphoreType.DMA((4,)),
        ],
        compiler_params=pltpu.CompilerParams(
            collective_id=0, has_side_effects=True, vmem_limit_bytes=56 << 20
        ),
    )(
        seed_field.reshape(4, 2, OWN, size),
        cotangent.reshape(2, 2, OWN, size),
        step_size,
        owner_list.reshape(1, size),
        lat_table,
        wave_table,
    )
    nonlinear, seed_next = pl.pallas_call(
        settle,
        out_shape=shapes,
        in_specs=[hbm] * 2,
        out_specs=(hbm, hbm),
        scratch_shapes=[
            pltpu.SemaphoreType.DMA((5,)),
        ],
        compiler_params=pltpu.CompilerParams(vmem_limit_bytes=40 << 20),
    )(*outputs)
    return (
        nonlinear.reshape(2, 1, 2, OWN, size),
        seed_next.reshape(4, 1, 2, OWN, size),
    )


def solution(mesh):
    split = P(None, "row", None, "ma", None)
    size = mesh.shape["ma"] * OWN
    lat_table = lat_constant(size)
    wave_table = wave_constant(size, 2 * size)
    body = jax.shard_map(
        local,
        mesh=mesh,
        in_specs=(P(), P(), split, split, P(), P()),
        out_specs=(split, split),
        check_vma=False,
    )

    def run(seed_field, cotangent, step_size, owner_list):
        return body(
            jnp.asarray(lat_table), jnp.asarray(wave_table), seed_field, cotangent, step_size, owner_list
        )

    return run
```

```python
import functools
import math

import jax
import jax.numpy as jnp
import numpy as np
from jax import lax
from jax.experimental import pallas as pl
from jax.experimental.pallas import tpu as pltpu
from jax.sharding import PartitionSpec as P

MESH = pl.DeviceIdType.MESH
LANES = 128
OWN = 32
F32 = jnp.float32
BF16 = jnp.bfloat16

NT = (((1,), (1,)), ((), ()))
NN = (((1,), (0,)), ((), ()))


def lat_constant(size):
    phase = (2 * np.arange(size)[:, None] + 1) * np.arange(size)[None, :] % (4 * size)
    return np.cos(phase * (math.pi / (2 * size))).astype(jnp.bfloat16)


def wave_constant(waves, points):
    phase = np.arange(waves)[:, None] * np.arange(points)[None, :] % points
    angles = phase * (2.0 * math.pi / points)
    return np.stack([np.cos(angles), -np.sin(angles)]).astype(jnp.bfloat16)


def dot(a, b, dims):
    return lax.dot_general(a, b, dims, preferred_element_type=F32)


def kernel(
    na,
    nr,
    seed_hbm,
    cot_hbm,
    step_hbm,
    owner_hbm,
    lat_hbm,
    wave_hbm,
    non_ref,
    next_ref,
    seed_ref,
    cot_ref,
    step_ref,
    owner_ref,
    lat,
    nat,
    table,
    onehot,
    owncol,
    mask,
    coef,
    listed,
    rows,
    grid,
    field,
    fwd_halo,
    back_send,
    back_halo,
    send,
    recv,
    load_sem,
    send_sem,
    recv_sem,
    halo_send_sem,
    halo_recv_sem,
):
    me = lax.axis_index("ma")
    radius = lax.axis_index("row")
    size = na * OWN
    points = 2 * size
    quads = na // 4
    chunk = min(256, size)
    tall = min(512, size)
    wide = min(1024, points)
    scale = 2.0 / size

    has_low = radius > 0
    has_high = radius < nr - 1
    barrier = pltpu.get_barrier_semaphore()

    loads = [
        pltpu.make_async_copy(src, dst, load_sem.at[i])
        for i, (src, dst) in enumerate(
            (
                (owner_hbm, owner_ref),
                (seed_hbm, seed_ref),
                (lat_hbm, lat),
                (cot_hbm, cot_ref),
                (step_hbm, step_ref),
                (wave_hbm, nat),
            )
        )
    ]
    load_owner, load_seed, load_lat, load_cot, load_step, load_wave = loads
    load_owner.start()
    load_seed.start()

    def greet(step, carry):
        peer = lax.rem(me + step, na)
        pl.semaphore_signal(barrier, inc=1, device_id={"ma": peer}, device_id_type=MESH)
        return carry

    lax.fori_loop(1, na, greet, 0)

    @pl.when(has_low)
    def _():
        pl.semaphore_signal(barrier, inc=1, device_id={"row": radius - 1}, device_id_type=MESH)

    @pl.when(has_high)
    def _():
        pl.semaphore_signal(barrier, inc=1, device_id={"row": radius + 1}, device_id_type=MESH)

    for load in loads[2:]:
        load.start()

    def scatter(k, first, count):
        def one(i, carry):
            peer = first + i
            block = send.at[k, pl.ds(pl.multiple_of(peer * OWN, OWN), OWN), :]

            @pl.when(peer != me)
            def _():
                pltpu.make_async_remote_copy(
                    src_ref=block,
                    dst_ref=recv.at[k, me],
                    send_sem=send_sem.at[k],
                    recv_sem=recv_sem.at[k],
                    device_id={"ma": peer},
                    device_id_type=MESH,
                ).start()

            @pl.when(peer == me)
            def _():
                recv[k, me] = block[...]

            return carry

        lax.fori_loop(0, count, one, 0)

    def ahead(k, first, count):
        def one(i, carry):
            peer = lax.rem(me + first + i, na)
            pltpu.make_async_remote_copy(
                src_ref=send.at[k, pl.ds(pl.multiple_of(peer * OWN, OWN), OWN), :],
                dst_ref=recv.at[k, me],
                send_sem=send_sem.at[k],
                recv_sem=recv_sem.at[k],
                device_id={"ma": peer},
                device_id_type=MESH,
            ).start()
            return carry

        lax.fori_loop(0, count, one, 0)

    def in_turn(k, height, rows_of, go=True):
        count = size // height
        peers = height // OWN

        def one(i, carry):
            turn = lax.rem(me // peers + i, count)
            at = pl.ds(pl.multiple_of(turn * height, height), height)
            send[k, at, :] = rows_of(at).astype(BF16)
            if go:
                scatter(k, turn * peers, peers)
            return carry

        lax.fori_loop(0, count, one, 0)

    def arrived(k):
        part = recv.at[k, pl.ds(0, na - 1)]
        pltpu.make_async_copy(part, part, recv_sem.at[k]).wait()

    def sent(k):
        part = send.at[k, pl.ds(0, (na - 1) * OWN), :]
        pltpu.make_async_copy(part, part, send_sem.at[k]).wait()

    def halo_copies(src, dst, base):
        down = pltpu.make_async_remote_copy(
            src_ref=src,
            dst_ref=dst.at[1],
            send_sem=halo_send_sem.at[base],
            recv_sem=halo_recv_sem.at[base + 1],
            device_id={"row": jnp.maximum(radius - 1, 0)},
            device_id_type=MESH,
        )
        up = pltpu.make_async_remote_copy(
            src_ref=src,
            dst_ref=dst.at[0],
            send_sem=halo_send_sem.at[base + 1],
            recv_sem=halo_recv_sem.at[base],
            device_id={"row": jnp.minimum(radius + 1, nr - 1)},
            device_id_type=MESH,
        )
        return down, up

    def halo_start(src, dst, base):
        height = src.shape[0] // 4

        def piece(i, carry):
            at = pl.ds(pl.multiple_of(i * height, height), height)
            down, up = halo_copies(src.at[at], dst.at[:, at], base)

            @pl.when(has_low)
            def _():
                down.start()

            @pl.when(has_high)
            def _():
                up.start()

            return carry

        lax.fori_loop(0, 4, piece, 0)

        @pl.when(jnp.logical_not(has_low))
        def _():
            dst[0] = jnp.zeros_like(dst[0])

        @pl.when(jnp.logical_not(has_high))
        def _():
            dst[1] = jnp.zeros_like(dst[1])

    def halo_wait(src, dst, base):
        down, up = halo_copies(src, dst, base)

        @pl.when(has_low)
        def _():
            up.wait_recv()

        @pl.when(has_high)
        def _():
            down.wait_recv()

    def halo_sent(src, dst, base):
        down, up = halo_copies(src, dst, base)

        @pl.when(has_low)
        def _():
            down.wait_send()

        @pl.when(has_high)
        def _():
            up.wait_send()

    group = lax.broadcasted_iota(jnp.int32, (OWN, LANES), 1) // OWN
    odd = lax.rem(group, 2) == 1
    high = group >= 2

    def regroup(k, put):
        def one(q, carry):
            x = [recv[k, 4 * q + a].astype(F32) for a in range(4)]
            y = [None] * 4
            for a in (0, 2):
                y[a] = jnp.where(odd, pltpu.roll(x[a + 1], 32, 1), x[a])
                y[a + 1] = jnp.where(odd, x[a + 1], pltpu.roll(x[a], 96, 1))
            z = [None] * 4
            for a in (0, 1):
                z[a] = jnp.where(high, pltpu.roll(y[a + 2], 64, 1), y[a])
                z[a + 2] = jnp.where(high, y[a + 2], pltpu.roll(y[a], 64, 1))
            columns = pl.ds(pl.multiple_of(q * LANES, LANES), LANES)
            for g in range(4):
                put(g, columns, z[g])
            return carry

        lax.fori_loop(0, quads, one, 0, unroll=min(4, quads))

    def stacked(k, left, height, go=True):
        in_turn(k, height, lambda at: dot(left[at, :], coef[...], NT), go)

    def order(at):
        for b in range(at.size // LANES):
            block = pl.ds(pl.multiple_of(at.start + b * LANES, LANES), LANES)
            column = jnp.transpose(jnp.broadcast_to(owner_ref[0:1, block], (LANES, LANES)))
            owncol[block, :] = column
            lane = lax.broadcasted_iota(jnp.int32, (LANES, LANES), 1)
            for c in range(size // LANES):
                onehot[block, c * LANES : (c + 1) * LANES] = jnp.where(
                    column == lane + c * LANES, 1.0, 0.0
                ).astype(BF16)

    def ordered(at):
        order(at)
        return dot(onehot[at, :], coef[...], NT)

    load_seed.wait()
    load_owner.wait()
    for k in range(2):
        for c in range(2):
            for s in range(2):
                g = 2 * c + s
                coef[g * OWN : (g + 1) * OWN, :] = seed_ref[k + 2 * c, s]
        if k == 0:
            pl.semaphore_wait(
                barrier, na - 1 + has_low.astype(jnp.int32) + has_high.astype(jnp.int32)
            )
            in_turn(k, chunk, ordered)
        else:
            stacked(k, onehot, chunk)

    mine = owncol[pl.ds(pl.multiple_of(me * OWN, OWN), OWN), :]
    for c in range(size // LANES):
        lane = lax.broadcasted_iota(jnp.int32, (OWN, LANES), 1) + c * LANES
        mask[:, c * LANES : (c + 1) * LANES] = jnp.where(lane >= mine, 1.0, 0.0)

    load_lat.wait()
    load_cot.wait()
    load_step.wait()
    for c in range(2):
        for s in range(2):
            g = 2 * c + s
            coef[g * OWN : (g + 1) * OWN, :] = jnp.where(
                mask[...] > 0.0, cot_ref[c, s].astype(F32), 0.0
            ).astype(BF16)
    stacked(4, lat, tall, go=False)

    load_wave.wait()
    part = min(512, points)
    wide_steps = points // part
    tall_steps = size // tall

    def permute(i, carry):
        s = i // (wide_steps * tall_steps)
        rest = lax.rem(i, wide_steps * tall_steps)
        columns = pl.ds(pl.multiple_of(lax.rem(rest, wide_steps) * part, part), part)
        top = pl.multiple_of((rest // wide_steps) * tall, tall)
        table[s, pl.ds(top, tall), columns] = dot(
            onehot[pl.ds(top, tall), :], nat[s, :, columns], NN
        ).astype(BF16)
        return carry

    lax.fori_loop(0, 2 * wide_steps * tall_steps, permute, 0)

    arrived(0)

    def keep_toroidal(g, columns, tile):
        listed[2 * (g // 2), g % 2, :, columns] = tile.astype(BF16)
        coef[g * OWN : (g + 1) * OWN, columns] = jnp.where(
            mask[:, columns] > 0.0, tile, 0.0
        ).astype(BF16)

    regroup(0, keep_toroidal)
    stacked(2, lat, chunk)

    near, some = na // 4, na // 8
    recv[4, me] = send[4, pl.ds(pl.multiple_of(me * OWN, OWN), OWN), :]
    ahead(4, near, some)
    ahead(4, na - near - some + 1, some)

    arrived(1)

    def keep_poloidal(g, columns, tile):
        listed[2 * (g // 2) + 1, g % 2, :, columns] = tile.astype(BF16)
        rows[g * OWN : (g + 1) * OWN, columns] = tile.astype(BF16)

    regroup(1, keep_poloidal)
    halo_start(rows, fwd_halo, 0)
    halo_wait(rows, fwd_halo, 0)
    for g in range(4):
        at = slice(g * OWN, (g + 1) * OWN)
        slope = 0.5 * (fwd_halo[1, at, :].astype(F32) - fwd_halo[0, at, :].astype(F32))
        coef[at, :] = jnp.where(mask[...] > 0.0, slope, 0.0).astype(BF16)
    stacked(3, lat, chunk)
    ahead(4, 1, near - 1)
    ahead(4, near + some, na - 2 * (near + some) + 1)
    ahead(4, na - near + 1, near - 1)

    def into_grid(base):
        def put(g, columns, tile):
            grid[base + g // 2, g % 2, :, columns] = tile.astype(BF16)

        return put

    arrived(2)
    regroup(2, into_grid(0))
    arrived(3)
    regroup(3, into_grid(2))

    def on_grid(first, count, columns):
        left = grid[first : first + count]
        total = None
        for s in range(2):
            part = dot(
                left[:, s].reshape(count * OWN, size), table[s, :, columns], NN
            )
            total = part if total is None else total + part
        total = total * scale
        return [total[c * OWN : (c + 1) * OWN] for c in range(count)]

    def terms(i, carry):
        columns = pl.ds(pl.multiple_of(i * wide, wide), wide)
        vel_tor, mag_tor, vel_pol, mag_pol = on_grid(0, 4, columns)
        for c, value in enumerate((vel_tor, mag_tor, vel_pol, mag_pol)):
            field[c, :, columns] = value
        back_send[0:OWN, columns] = (mag_tor * mag_pol - vel_tor * vel_pol).astype(BF16)
        back_send[OWN : 2 * OWN, columns] = (vel_tor * mag_pol - vel_pol * mag_tor).astype(BF16)
        return carry

    def analyse(k, source):
        def made(at):
            parts = [dot(table[s, at, :], source[...], NT) for s in range(2)]
            return scale * jnp.concatenate(parts, axis=1)

        in_turn(k, tall, made)

    lax.fori_loop(0, points // wide, terms, 0)
    analyse(5, back_send)

    arrived(4)
    regroup(4, into_grid(4))
    tor_grad = back_halo.at[2]

    def grads(i, carry):
        columns = pl.ds(pl.multiple_of(i * wide, wide), wide)
        adj_vel, adj_mag = on_grid(4, 2, columns)
        vel_tor, mag_tor, vel_pol, mag_pol = (field[c, :, columns] for c in range(4))
        back_send[0:OWN, columns] = (-vel_tor * adj_vel - mag_tor * adj_mag).astype(BF16)
        back_send[OWN : 2 * OWN, columns] = (mag_tor * adj_vel + vel_tor * adj_mag).astype(BF16)
        tor_grad[0:OWN, columns] = (-vel_pol * adj_vel + mag_pol * adj_mag).astype(BF16)
        tor_grad[OWN : 2 * OWN, columns] = (mag_pol * adj_vel - vel_pol * adj_mag).astype(BF16)
        return carry

    lax.fori_loop(0, points // wide, grads, 0)
    halo_start(back_send, back_halo, 2)
    analyse(6, tor_grad)
    halo_wait(back_send, back_halo, 2)
    tor_grad[...] = (
        0.5 * (back_halo[0].astype(F32) - back_halo[1].astype(F32))
    ).astype(BF16)
    analyse(7, tor_grad)

    step = jnp.broadcast_to(step_ref[...].reshape(1, 1), (OWN, chunk))

    def finish(k, put):
        arrived(k)

        def keep(g, columns, tile):
            rows[g * OWN : (g + 1) * OWN, columns] = tile.astype(BF16)

        if k == 5:
            halo_sent(rows, fwd_halo, 0)
        regroup(k, keep)

        def one(i, carry):
            columns = pl.ds(pl.multiple_of(i * chunk, chunk), chunk)
            result = dot(rows[...], lat[:, columns], NN)
            live = mask[:, columns] > 0.0
            for g in range(4):
                put(
                    g // 2,
                    g % 2,
                    columns,
                    jnp.where(live, result[g * OWN : (g + 1) * OWN], 0.0),
                )
            return carry

        lax.fori_loop(0, size // chunk, one, 0)

    def put_term(s, c, columns, value):
        non_ref[c, s, :, columns] = value

    def put_seed(first):
        def put(s, c, columns, value):
            channel = 2 * c + first
            next_ref[channel, s, :, columns] = (
                listed[channel, s, :, columns].astype(F32) - step * value
            )

        return put

    finish(5, put_term)
    finish(6, put_seed(0))
    finish(7, put_seed(1))
    halo_sent(back_send, back_halo, 2)
    for k in range(8):
        sent(k)


def settle(non_in, next_in, non_out, next_out, store_sem):
    stores = [pltpu.make_async_copy(non_in, non_out, store_sem.at[0])]
    for channel in range(4):
        stores.append(
            pltpu.make_async_copy(
                next_in.at[channel], next_out.at[channel], store_sem.at[channel + 1]
            )
        )
    for store in stores:
        store.start()
    for store in stores:
        store.wait()


def local(lat_table, wave_table, seed_field, cotangent, step_size, owner_list):
    na = lax.axis_size("ma")
    nr = lax.axis_size("row")
    size = na * OWN
    points = 2 * size
    hbm = pl.BlockSpec(memory_space=pl.ANY)
    shapes = (
        jax.ShapeDtypeStruct((2, 2, OWN, size), F32),
        jax.ShapeDtypeStruct((4, 2, OWN, size), F32),
    )
    outputs = pl.pallas_call(
        functools.partial(kernel, na, nr),
        out_shape=(pltpu.VMEM(shapes[0].shape, F32), pltpu.VMEM(shapes[1].shape, F32)),
        in_specs=[pl.BlockSpec(memory_space=pltpu.HBM)] * 6,
        out_specs=(pl.BlockSpec(memory_space=pltpu.VMEM),) * 2,
        scratch_shapes=[
            pltpu.VMEM((4, 2, OWN, size), BF16),
            pltpu.VMEM((2, 2, OWN, size), BF16),
            pltpu.VMEM((1,), F32),
            pltpu.VMEM((1, size), jnp.int32),
            pltpu.VMEM((size, size), BF16),
            pltpu.VMEM((2, size, points), BF16),
            pltpu.VMEM((2, size, points), BF16),
            pltpu.VMEM((size, size), BF16),
            pltpu.VMEM((size, LANES), jnp.int32),
            pltpu.VMEM((OWN, size), F32),
            pltpu.VMEM((4 * OWN, size), BF16),
            pltpu.VMEM((4, 2, OWN, size), BF16),
            pltpu.VMEM((4 * OWN, size), BF16),
            pltpu.VMEM((6, 2, OWN, size), BF16),
            pltpu.VMEM((4, OWN, points), F32),
            pltpu.VMEM((2, 4 * OWN, size), BF16),
            pltpu.VMEM((2 * OWN, points), BF16),
            pltpu.VMEM((3, 2 * OWN, points), BF16),
            pltpu.VMEM((8, size, LANES), BF16),
            pltpu.VMEM((8, na, OWN, LANES), BF16),
            pltpu.SemaphoreType.DMA((6,)),
            pltpu.SemaphoreType.DMA((8,)),
            pltpu.SemaphoreType.DMA((8,)),
            pltpu.SemaphoreType.DMA((4,)),
            pltpu.SemaphoreType.DMA((4,)),
        ],
        compiler_params=pltpu.CompilerParams(
            collective_id=0, has_side_effects=True, vmem_limit_bytes=56 << 20
        ),
    )(
        seed_field.reshape(4, 2, OWN, size),
        cotangent.reshape(2, 2, OWN, size),
        step_size,
        owner_list.reshape(1, size),
        lat_table,
        wave_table,
    )
    nonlinear, seed_next = pl.pallas_call(
        settle,
        out_shape=shapes,
        in_specs=[hbm] * 2,
        out_specs=(hbm, hbm),
        scratch_shapes=[
            pltpu.SemaphoreType.DMA((5,)),
        ],
        compiler_params=pltpu.CompilerParams(vmem_limit_bytes=40 << 20),
    )(*outputs)
    return (
        nonlinear.reshape(2, 1, 2, OWN, size),
        seed_next.reshape(4, 1, 2, OWN, size),
    )


def solution(mesh):
    split = P(None, "row", None, "ma", None)
    size = mesh.shape["ma"] * OWN
    lat_table = lat_constant(size)
    wave_table = wave_constant(size, 2 * size)
    body = jax.shard_map(
        local,
        mesh=mesh,
        in_specs=(P(), P(), split, split, P(), P()),
        out_specs=(split, split),
        check_vma=False,
    )

    def run(seed_field, cotangent, step_size, owner_list):
        return body(
            jnp.asarray(lat_table), jnp.asarray(wave_table), seed_field, cotangent, step_size, owner_list
        )

    return run
```

```python
import functools
import math

import jax
import jax.numpy as jnp
import numpy as np
from jax import lax
from jax.experimental import pallas as pl
from jax.experimental.pallas import tpu as pltpu
from jax.sharding import PartitionSpec as P

MESH = pl.DeviceIdType.MESH
LANES = 128
OWN = 32
F32 = jnp.float32
BF16 = jnp.bfloat16

NT = (((1,), (1,)), ((), ()))
NN = (((1,), (0,)), ((), ()))


def lat_constant(size):
    phase = (2 * np.arange(size)[:, None] + 1) * np.arange(size)[None, :] % (4 * size)
    return np.cos(phase * (math.pi / (2 * size))).astype(jnp.bfloat16)


def wave_constant(waves, points):
    phase = np.arange(waves)[:, None] * np.arange(points)[None, :] % points
    angles = phase * (2.0 * math.pi / points)
    return np.stack([np.cos(angles), -np.sin(angles)]).astype(jnp.bfloat16)


def dot(a, b, dims):
    return lax.dot_general(a, b, dims, preferred_element_type=F32)


def kernel(
    na,
    nr,
    seed_hbm,
    cot_hbm,
    step_hbm,
    owner_hbm,
    lat_hbm,
    wave_hbm,
    non_ref,
    next_ref,
    seed_ref,
    cot_ref,
    step_ref,
    owner_ref,
    lat,
    nat,
    table,
    onehot,
    owncol,
    mask,
    coef,
    listed,
    rows,
    grid,
    field,
    fwd_halo,
    back_send,
    back_halo,
    send,
    recv,
    load_sem,
    send_sem,
    recv_sem,
    halo_send_sem,
    halo_recv_sem,
):
    me = lax.axis_index("ma")
    radius = lax.axis_index("row")
    size = na * OWN
    points = 2 * size
    quads = na // 4
    chunk = min(256, size)
    tall = min(512, size)
    wide = min(1024, points)
    scale = 2.0 / size

    has_low = radius > 0
    has_high = radius < nr - 1
    barrier = pltpu.get_barrier_semaphore()

    loads = [
        pltpu.make_async_copy(src, dst, load_sem.at[i])
        for i, (src, dst) in enumerate(
            (
                (owner_hbm, owner_ref),
                (seed_hbm, seed_ref),
                (lat_hbm, lat),
                (cot_hbm, cot_ref),
                (step_hbm, step_ref),
                (wave_hbm, nat),
            )
        )
    ]
    load_owner, load_seed, load_lat, load_cot, load_step, load_wave = loads
    load_owner.start()
    load_seed.start()

    def greet(i, carry):
        peer = lax.rem(me + na // 2 + (i + 1) // 2 * (1 - 2 * lax.rem(i, 2)), na)
        pl.semaphore_signal(barrier, inc=1, device_id={"ma": peer}, device_id_type=MESH)
        return carry

    lax.fori_loop(0, na - 1, greet, 0)

    @pl.when(has_low)
    def _():
        pl.semaphore_signal(barrier, inc=1, device_id={"row": radius - 1}, device_id_type=MESH)

    @pl.when(has_high)
    def _():
        pl.semaphore_signal(barrier, inc=1, device_id={"row": radius + 1}, device_id_type=MESH)

    for load in loads[2:]:
        load.start()

    def scatter(k, first, count):
        def one(i, carry):
            peer = first + i
            block = send.at[k, pl.ds(pl.multiple_of(peer * OWN, OWN), OWN), :]

            @pl.when(peer != me)
            def _():
                pltpu.make_async_remote_copy(
                    src_ref=block,
                    dst_ref=recv.at[k, me],
                    send_sem=send_sem.at[k],
                    recv_sem=recv_sem.at[k],
                    device_id={"ma": peer},
                    device_id_type=MESH,
                ).start()

            @pl.when(peer == me)
            def _():
                recv[k, me] = block[...]

            return carry

        lax.fori_loop(0, count, one, 0)

    def ahead(k, first, count):
        def one(i, carry):
            peer = lax.rem(me + first + i, na)
            pltpu.make_async_remote_copy(
                src_ref=send.at[k, pl.ds(pl.multiple_of(peer * OWN, OWN), OWN), :],
                dst_ref=recv.at[k, me],
                send_sem=send_sem.at[k],
                recv_sem=recv_sem.at[k],
                device_id={"ma": peer},
                device_id_type=MESH,
            ).start()
            return carry

        lax.fori_loop(0, count, one, 0)

    def in_turn(k, height, rows_of, go=True):
        count = size // height
        peers = height // OWN

        def one(i, carry):
            turn = lax.rem(me // peers + count // 2 + i + i * (i - 1) // 2, count)
            at = pl.ds(pl.multiple_of(turn * height, height), height)
            send[k, at, :] = rows_of(at).astype(BF16)
            if go:
                scatter(k, turn * peers, peers)
            return carry

        lax.fori_loop(0, count, one, 0)

    def arrived(k):
        part = recv.at[k, pl.ds(0, na - 1)]
        pltpu.make_async_copy(part, part, recv_sem.at[k]).wait()

    def sent(k):
        part = send.at[k, pl.ds(0, (na - 1) * OWN), :]
        pltpu.make_async_copy(part, part, send_sem.at[k]).wait()

    def halo_copies(src, dst, base):
        down = pltpu.make_async_remote_copy(
            src_ref=src,
            dst_ref=dst.at[1],
            send_sem=halo_send_sem.at[base],
            recv_sem=halo_recv_sem.at[base + 1],
            device_id={"row": jnp.maximum(radius - 1, 0)},
            device_id_type=MESH,
        )
        up = pltpu.make_async_remote_copy(
            src_ref=src,
            dst_ref=dst.at[0],
            send_sem=halo_send_sem.at[base + 1],
            recv_sem=halo_recv_sem.at[base],
            device_id={"row": jnp.minimum(radius + 1, nr - 1)},
            device_id_type=MESH,
        )
        return down, up

    def halo_start(src, dst, base):
        height = src.shape[0] // 4

        def piece(i, carry):
            at = pl.ds(pl.multiple_of(i * height, height), height)
            down, up = halo_copies(src.at[at], dst.at[:, at], base)

            @pl.when(has_low)
            def _():
                down.start()

            @pl.when(has_high)
            def _():
                up.start()

            return carry

        lax.fori_loop(0, 4, piece, 0)

        @pl.when(jnp.logical_not(has_low))
        def _():
            dst[0] = jnp.zeros_like(dst[0])

        @pl.when(jnp.logical_not(has_high))
        def _():
            dst[1] = jnp.zeros_like(dst[1])

    def halo_wait(src, dst, base):
        down, up = halo_copies(src, dst, base)

        @pl.when(has_low)
        def _():
            up.wait_recv()

        @pl.when(has_high)
        def _():
            down.wait_recv()

    def halo_sent(src, dst, base):
        down, up = halo_copies(src, dst, base)

        @pl.when(has_low)
        def _():
            down.wait_send()

        @pl.when(has_high)
        def _():
            up.wait_send()

    group = lax.broadcasted_iota(jnp.int32, (OWN, LANES), 1) // OWN
    odd = lax.rem(group, 2) == 1
    high = group >= 2

    def regroup(k, put):
        def one(q, carry):
            x = [recv[k, 4 * q + a].astype(F32) for a in range(4)]
            y = [None] * 4
            for a in (0, 2):
                y[a] = jnp.where(odd, pltpu.roll(x[a + 1], 32, 1), x[a])
                y[a + 1] = jnp.where(odd, x[a + 1], pltpu.roll(x[a], 96, 1))
            z = [None] * 4
            for a in (0, 1):
                z[a] = jnp.where(high, pltpu.roll(y[a + 2], 64, 1), y[a])
                z[a + 2] = jnp.where(high, y[a + 2], pltpu.roll(y[a], 64, 1))
            columns = pl.ds(pl.multiple_of(q * LANES, LANES), LANES)
            for g in range(4):
                put(g, columns, z[g])
            return carry

        lax.fori_loop(0, quads, one, 0, unroll=min(4, quads))

    def stacked(k, left, height, go=True):
        in_turn(k, height, lambda at: dot(left[at, :], coef[...], NT), go)

    def order(at):
        for b in range(at.size // LANES):
            block = pl.ds(pl.multiple_of(at.start + b * LANES, LANES), LANES)
            column = jnp.transpose(jnp.broadcast_to(owner_ref[0:1, block], (LANES, LANES)))
            owncol[block, :] = column
            lane = lax.broadcasted_iota(jnp.int32, (LANES, LANES), 1)
            for c in range(size // LANES):
                onehot[block, c * LANES : (c + 1) * LANES] = jnp.where(
                    column == lane + c * LANES, 1.0, 0.0
                ).astype(BF16)

    def ordered(at):
        order(at)
        return dot(onehot[at, :], coef[...], NT)

    load_seed.wait()
    load_owner.wait()
    for k in range(2):
        for c in range(2):
            for s in range(2):
                g = 2 * c + s
                coef[g * OWN : (g + 1) * OWN, :] = seed_ref[k + 2 * c, s]
        if k == 0:
            pl.semaphore_wait(
                barrier, na - 1 + has_low.astype(jnp.int32) + has_high.astype(jnp.int32)
            )
            in_turn(k, chunk, ordered)
        else:
            stacked(k, onehot, chunk)

    mine = owncol[pl.ds(pl.multiple_of(me * OWN, OWN), OWN), :]
    for c in range(size // LANES):
        lane = lax.broadcasted_iota(jnp.int32, (OWN, LANES), 1) + c * LANES
        mask[:, c * LANES : (c + 1) * LANES] = jnp.where(lane >= mine, 1.0, 0.0)

    load_lat.wait()
    load_cot.wait()
    load_step.wait()
    for c in range(2):
        for s in range(2):
            g = 2 * c + s
            coef[g * OWN : (g + 1) * OWN, :] = jnp.where(
                mask[...] > 0.0, cot_ref[c, s].astype(F32), 0.0
            ).astype(BF16)
    stacked(4, lat, tall, go=False)

    load_wave.wait()
    part = min(512, points)
    wide_steps = points // part
    tall_steps = size // tall

    def permute(i, carry):
        s = i // (wide_steps * tall_steps)
        rest = lax.rem(i, wide_steps * tall_steps)
        columns = pl.ds(pl.multiple_of(lax.rem(rest, wide_steps) * part, part), part)
        top = pl.multiple_of((rest // wide_steps) * tall, tall)
        table[s, pl.ds(top, tall), columns] = dot(
            onehot[pl.ds(top, tall), :], nat[s, :, columns], NN
        ).astype(BF16)
        return carry

    lax.fori_loop(0, 2 * wide_steps * tall_steps, permute, 0)

    arrived(0)

    def keep_toroidal(g, columns, tile):
        listed[2 * (g // 2), g % 2, :, columns] = tile.astype(BF16)
        coef[g * OWN : (g + 1) * OWN, columns] = jnp.where(
            mask[:, columns] > 0.0, tile, 0.0
        ).astype(BF16)

    regroup(0, keep_toroidal)
    stacked(2, lat, chunk)

    near, some = na // 4, na // 8
    recv[4, me] = send[4, pl.ds(pl.multiple_of(me * OWN, OWN), OWN), :]
    ahead(4, near, some)
    ahead(4, na - near - some + 1, some)

    arrived(1)

    def keep_poloidal(g, columns, tile):
        listed[2 * (g // 2) + 1, g % 2, :, columns] = tile.astype(BF16)
        rows[g * OWN : (g + 1) * OWN, columns] = tile.astype(BF16)

    regroup(1, keep_poloidal)
    halo_start(rows, fwd_halo, 0)
    halo_wait(rows, fwd_halo, 0)
    for g in range(4):
        at = slice(g * OWN, (g + 1) * OWN)
        slope = 0.5 * (fwd_halo[1, at, :].astype(F32) - fwd_halo[0, at, :].astype(F32))
        coef[at, :] = jnp.where(mask[...] > 0.0, slope, 0.0).astype(BF16)
    stacked(3, lat, chunk)
    ahead(4, 1, near - 1)
    ahead(4, near + some, na - 2 * (near + some) + 1)
    ahead(4, na - near + 1, near - 1)

    def into_grid(base):
        def put(g, columns, tile):
            grid[base + g // 2, g % 2, :, columns] = tile.astype(BF16)

        return put

    arrived(2)
    regroup(2, into_grid(0))
    arrived(3)
    regroup(3, into_grid(2))

    def on_grid(first, count, columns):
        left = grid[first : first + count]
        total = None
        for s in range(2):
            part = dot(
                left[:, s].reshape(count * OWN, size), table[s, :, columns], NN
            )
            total = part if total is None else total + part
        total = total * scale
        return [total[c * OWN : (c + 1) * OWN] for c in range(count)]

    def terms(i, carry):
        columns = pl.ds(pl.multiple_of(i * wide, wide), wide)
        vel_tor, mag_tor, vel_pol, mag_pol = on_grid(0, 4, columns)
        for c, value in enumerate((vel_tor, mag_tor, vel_pol, mag_pol)):
            field[c, :, columns] = value
        back_send[0:OWN, columns] = (mag_tor * mag_pol - vel_tor * vel_pol).astype(BF16)
        back_send[OWN : 2 * OWN, columns] = (vel_tor * mag_pol - vel_pol * mag_tor).astype(BF16)
        return carry

    def analyse(k, source):
        def made(at):
            parts = [dot(table[s, at, :], source[...], NT) for s in range(2)]
            return scale * jnp.concatenate(parts, axis=1)

        in_turn(k, tall, made)

    lax.fori_loop(0, points // wide, terms, 0)
    analyse(5, back_send)

    arrived(4)
    regroup(4, into_grid(4))
    tor_grad = back_halo.at[2]

    def grads(i, carry):
        columns = pl.ds(pl.multiple_of(i * wide, wide), wide)
        adj_vel, adj_mag = on_grid(4, 2, columns)
        vel_tor, mag_tor, vel_pol, mag_pol = (field[c, :, columns] for c in range(4))
        back_send[0:OWN, columns] = (-vel_tor * adj_vel - mag_tor * adj_mag).astype(BF16)
        back_send[OWN : 2 * OWN, columns] = (mag_tor * adj_vel + vel_tor * adj_mag).astype(BF16)
        tor_grad[0:OWN, columns] = (-vel_pol * adj_vel + mag_pol * adj_mag).astype(BF16)
        tor_grad[OWN : 2 * OWN, columns] = (mag_pol * adj_vel - vel_pol * adj_mag).astype(BF16)
        return carry

    lax.fori_loop(0, points // wide, grads, 0)
    halo_start(back_send, back_halo, 2)
    analyse(6, tor_grad)
    halo_wait(back_send, back_halo, 2)
    tor_grad[...] = (
        0.5 * (back_halo[0].astype(F32) - back_halo[1].astype(F32))
    ).astype(BF16)
    analyse(7, tor_grad)

    step = jnp.broadcast_to(step_ref[...].reshape(1, 1), (OWN, size))

    def finish(k, put):
        arrived(k)

        def keep(g, columns, tile):
            rows[g * OWN : (g + 1) * OWN, columns] = tile.astype(BF16)

        if k == 5:
            halo_sent(rows, fwd_halo, 0)
        regroup(k, keep)

        result = dot(rows[...], lat[...], NN)
        live = mask[...] > 0.0
        for g in range(4):
            put(g // 2, g % 2, jnp.where(live, result[g * OWN : (g + 1) * OWN], 0.0))

    def put_term(s, c, value):
        non_ref[c, s] = value

    def put_seed(first):
        def put(s, c, value):
            channel = 2 * c + first
            next_ref[channel, s] = listed[channel, s].astype(F32) - step * value

        return put

    finish(5, put_term)
    finish(6, put_seed(0))
    finish(7, put_seed(1))
    halo_sent(back_send, back_halo, 2)
    for k in range(8):
        sent(k)


def settle(non_in, next_in, non_out, next_out, store_sem):
    stores = []
    for src, dst in ((next_in, next_out), (non_in, non_out)):
        for c in range(src.shape[0]):
            for s in range(2):
                stores.append(
                    pltpu.make_async_copy(src.at[c, s], dst.at[c, s], store_sem.at[len(stores)])
                )
    for store in stores:
        store.start()
    for store in stores:
        store.wait()


def local(lat_table, wave_table, seed_field, cotangent, step_size, owner_list):
    na = lax.axis_size("ma")
    nr = lax.axis_size("row")
    size = na * OWN
    points = 2 * size
    hbm = pl.BlockSpec(memory_space=pl.ANY)
    shapes = (
        jax.ShapeDtypeStruct((2, 2, OWN, size), F32),
        jax.ShapeDtypeStruct((4, 2, OWN, size), F32),
    )
    outputs = pl.pallas_call(
        functools.partial(kernel, na, nr),
        out_shape=(pltpu.VMEM(shapes[0].shape, F32), pltpu.VMEM(shapes[1].shape, F32)),
        in_specs=[pl.BlockSpec(memory_space=pltpu.HBM)] * 6,
        out_specs=(pl.BlockSpec(memory_space=pltpu.VMEM),) * 2,
        scratch_shapes=[
            pltpu.VMEM((4, 2, OWN, size), BF16),
            pltpu.VMEM((2, 2, OWN, size), BF16),
            pltpu.VMEM((1,), F32),
            pltpu.VMEM((1, size), jnp.int32),
            pltpu.VMEM((size, size), BF16),
            pltpu.VMEM((2, size, points), BF16),
            pltpu.VMEM((2, size, points), BF16),
            pltpu.VMEM((size, size), BF16),
            pltpu.VMEM((size, LANES), jnp.int32),
            pltpu.VMEM((OWN, size), F32),
            pltpu.VMEM((4 * OWN, size), BF16),
            pltpu.VMEM((4, 2, OWN, size), BF16),
            pltpu.VMEM((4 * OWN, size), BF16),
            pltpu.VMEM((6, 2, OWN, size), BF16),
            pltpu.VMEM((4, OWN, points), F32),
            pltpu.VMEM((2, 4 * OWN, size), BF16),
            pltpu.VMEM((2 * OWN, points), BF16),
            pltpu.VMEM((3, 2 * OWN, points), BF16),
            pltpu.VMEM((8, size, LANES), BF16),
            pltpu.VMEM((8, na, OWN, LANES), BF16),
            pltpu.SemaphoreType.DMA((6,)),
            pltpu.SemaphoreType.DMA((8,)),
            pltpu.SemaphoreType.DMA((8,)),
            pltpu.SemaphoreType.DMA((4,)),
            pltpu.SemaphoreType.DMA((4,)),
        ],
        compiler_params=pltpu.CompilerParams(
            collective_id=0, has_side_effects=True, vmem_limit_bytes=56 << 20
        ),
    )(
        seed_field.reshape(4, 2, OWN, size),
        cotangent.reshape(2, 2, OWN, size),
        step_size,
        owner_list.reshape(1, size),
        lat_table,
        wave_table,
    )
    nonlinear, seed_next = pl.pallas_call(
        settle,
        out_shape=shapes,
        in_specs=[hbm] * 2,
        out_specs=(hbm, hbm),
        scratch_shapes=[
            pltpu.SemaphoreType.DMA((12,)),
        ],
        compiler_params=pltpu.CompilerParams(vmem_limit_bytes=40 << 20),
    )(*outputs)
    return (
        nonlinear.reshape(2, 1, 2, OWN, size),
        seed_next.reshape(4, 1, 2, OWN, size),
    )


def solution(mesh):
    split = P(None, "row", None, "ma", None)
    size = mesh.shape["ma"] * OWN
    lat_table = lat_constant(size)
    wave_table = wave_constant(size, 2 * size)
    body = jax.shard_map(
        local,
        mesh=mesh,
        in_specs=(P(), P(), split, split, P(), P()),
        out_specs=(split, split),
        check_vma=False,
    )

    def run(seed_field, cotangent, step_size, owner_list):
        return body(
            jnp.asarray(lat_table), jnp.asarray(wave_table), seed_field, cotangent, step_size, owner_list
        )

    return run
```

```python
import functools
import math

import jax
import jax.numpy as jnp
import numpy as np
from jax import lax
from jax.experimental import pallas as pl
from jax.experimental.pallas import tpu as pltpu
from jax.sharding import PartitionSpec as P

MESH = pl.DeviceIdType.MESH
LANES = 128
OWN = 32
F32 = jnp.float32
BF16 = jnp.bfloat16

NT = (((1,), (1,)), ((), ()))
NN = (((1,), (0,)), ((), ()))


def lat_constant(size):
    phase = (2 * np.arange(size)[:, None] + 1) * np.arange(size)[None, :] % (4 * size)
    return np.cos(phase * (math.pi / (2 * size))).astype(jnp.bfloat16)


def wave_constant(waves, points):
    phase = np.arange(waves)[:, None] * np.arange(points)[None, :] % points
    angles = phase * (2.0 * math.pi / points)
    return np.stack([np.cos(angles), -np.sin(angles)]).astype(jnp.bfloat16)


def dot(a, b, dims):
    return lax.dot_general(a, b, dims, preferred_element_type=F32)


def kernel(
    na,
    nr,
    seed_hbm,
    cot_hbm,
    step_hbm,
    owner_hbm,
    lat_hbm,
    wave_hbm,
    non_ref,
    next_ref,
    seed_ref,
    cot_ref,
    step_ref,
    owner_ref,
    lat,
    nat,
    table,
    onehot,
    owncol,
    mask,
    coef,
    listed,
    rows,
    grid,
    field,
    fwd_halo,
    back_send,
    back_halo,
    send,
    recv,
    load_sem,
    send_sem,
    recv_sem,
    halo_send_sem,
    halo_recv_sem,
):
    me = lax.axis_index("ma")
    radius = lax.axis_index("row")
    size = na * OWN
    points = 2 * size
    quads = na // 4
    chunk = min(256, size)
    tall = min(512, size)
    wide = min(1024, points)
    scale = 2.0 / size

    has_low = radius > 0
    has_high = radius < nr - 1
    barrier = pltpu.get_barrier_semaphore()

    loads = [
        pltpu.make_async_copy(src, dst, load_sem.at[i])
        for i, (src, dst) in enumerate(
            (
                (owner_hbm, owner_ref),
                (seed_hbm, seed_ref),
                (lat_hbm, lat),
                (cot_hbm, cot_ref),
                (step_hbm, step_ref),
                (wave_hbm, nat),
            )
        )
    ]
    load_owner, load_seed, load_lat, load_cot, load_step, load_wave = loads
    load_owner.start()
    load_seed.start()

    def farthest(i):
        return lax.rem(me + na // 2 + (i + 1) // 2 * (1 - 2 * lax.rem(i, 2)), na)

    def greet(i, carry):
        pl.semaphore_signal(barrier, inc=1, device_id={"ma": farthest(i)}, device_id_type=MESH)
        return carry

    lax.fori_loop(0, na - 1, greet, 0)

    @pl.when(has_low)
    def _():
        pl.semaphore_signal(barrier, inc=1, device_id={"row": radius - 1}, device_id_type=MESH)

    @pl.when(has_high)
    def _():
        pl.semaphore_signal(barrier, inc=1, device_id={"row": radius + 1}, device_id_type=MESH)

    for load in loads[2:]:
        load.start()

    def send_block(k, peer):
        pltpu.make_async_remote_copy(
            src_ref=send.at[k, pl.ds(pl.multiple_of(peer * OWN, OWN), OWN), :],
            dst_ref=recv.at[k, me],
            send_sem=send_sem.at[k],
            recv_sem=recv_sem.at[k],
            device_id={"ma": peer},
            device_id_type=MESH,
        ).start()

    def keep_own(k):
        recv[k, me] = send[k, pl.ds(pl.multiple_of(me * OWN, OWN), OWN), :]

    def scatter(k, first, last):
        def one(i, carry):
            send_block(k, farthest(i))
            return carry

        lax.fori_loop(first, last, one, 0)

    def made(k, height, rows_of):
        def one(i, carry):
            at = pl.ds(pl.multiple_of(i * height, height), height)
            send[k, at, :] = rows_of(at).astype(BF16)
            return carry

        lax.fori_loop(0, size // height, one, 0)
        keep_own(k)

    def made_in_turn(k, height, rows_of):
        count = size // height
        peers = height // OWN

        def one(i, carry):
            turn = lax.rem(me // peers + count // 2 + i + i * (i - 1) // 2, count)
            at = pl.ds(pl.multiple_of(turn * height, height), height)
            send[k, at, :] = rows_of(at).astype(BF16)

            def block(j, carry):
                peer = turn * peers + j

                @pl.when(peer != me)
                def _():
                    send_block(k, peer)

                return carry

            lax.fori_loop(0, peers, block, 0)
            return carry

        lax.fori_loop(0, count, one, 0)
        keep_own(k)

    def arrived(k):
        part = recv.at[k, pl.ds(0, na - 1)]
        pltpu.make_async_copy(part, part, recv_sem.at[k]).wait()

    def sent(k):
        part = send.at[k, pl.ds(0, (na - 1) * OWN), :]
        pltpu.make_async_copy(part, part, send_sem.at[k]).wait()

    def halo_copies(src, dst, base):
        down = pltpu.make_async_remote_copy(
            src_ref=src,
            dst_ref=dst.at[1],
            send_sem=halo_send_sem.at[base],
            recv_sem=halo_recv_sem.at[base + 1],
            device_id={"row": jnp.maximum(radius - 1, 0)},
            device_id_type=MESH,
        )
        up = pltpu.make_async_remote_copy(
            src_ref=src,
            dst_ref=dst.at[0],
            send_sem=halo_send_sem.at[base + 1],
            recv_sem=halo_recv_sem.at[base],
            device_id={"row": jnp.minimum(radius + 1, nr - 1)},
            device_id_type=MESH,
        )
        return down, up

    def halo_start(src, dst, base):
        height = src.shape[0] // 4

        def piece(i, carry):
            at = pl.ds(pl.multiple_of(i * height, height), height)
            down, up = halo_copies(src.at[at], dst.at[:, at], base)

            @pl.when(has_low)
            def _():
                down.start()

            @pl.when(has_high)
            def _():
                up.start()

            return carry

        lax.fori_loop(0, 4, piece, 0)

        @pl.when(jnp.logical_not(has_low))
        def _():
            dst[0] = jnp.zeros_like(dst[0])

        @pl.when(jnp.logical_not(has_high))
        def _():
            dst[1] = jnp.zeros_like(dst[1])

    def halo_wait(src, dst, base):
        down, up = halo_copies(src, dst, base)

        @pl.when(has_low)
        def _():
            up.wait_recv()

        @pl.when(has_high)
        def _():
            down.wait_recv()

    def halo_sent(src, dst, base):
        down, up = halo_copies(src, dst, base)

        @pl.when(has_low)
        def _():
            down.wait_send()

        @pl.when(has_high)
        def _():
            up.wait_send()

    group = lax.broadcasted_iota(jnp.int32, (OWN, LANES), 1) // OWN
    odd = lax.rem(group, 2) == 1
    high = group >= 2

    def regroup(k, put):
        def one(q, carry):
            x = [recv[k, 4 * q + a].astype(F32) for a in range(4)]
            y = [None] * 4
            for a in (0, 2):
                y[a] = jnp.where(odd, pltpu.roll(x[a + 1], 32, 1), x[a])
                y[a + 1] = jnp.where(odd, x[a + 1], pltpu.roll(x[a], 96, 1))
            z = [None] * 4
            for a in (0, 1):
                z[a] = jnp.where(high, pltpu.roll(y[a + 2], 64, 1), y[a])
                z[a + 2] = jnp.where(high, y[a + 2], pltpu.roll(y[a], 64, 1))
            columns = pl.ds(pl.multiple_of(q * LANES, LANES), LANES)
            for g in range(4):
                put(g, columns, z[g])
            return carry

        lax.fori_loop(0, quads, one, 0, unroll=min(4, quads))

    def stacked(k, left):
        made(k, tall, lambda at: dot(left[at, :], coef[...], NT))

    def order(at):
        for b in range(at.size // LANES):
            block = pl.ds(pl.multiple_of(at.start + b * LANES, LANES), LANES)
            column = jnp.transpose(jnp.broadcast_to(owner_ref[0:1, block], (LANES, LANES)))
            owncol[block, :] = column
            lane = lax.broadcasted_iota(jnp.int32, (LANES, LANES), 1)
            for c in range(size // LANES):
                onehot[block, c * LANES : (c + 1) * LANES] = jnp.where(
                    column == lane + c * LANES, 1.0, 0.0
                ).astype(BF16)

    def ordered(at):
        order(at)
        return dot(onehot[at, :], coef[...], NT)

    load_seed.wait()
    load_owner.wait()
    for k in range(2):
        for c in range(2):
            for s in range(2):
                g = 2 * c + s
                coef[g * OWN : (g + 1) * OWN, :] = seed_ref[k + 2 * c, s]
        if k == 0:
            pl.semaphore_wait(
                barrier, na - 1 + has_low.astype(jnp.int32) + has_high.astype(jnp.int32)
            )
            made_in_turn(k, chunk, ordered)
        else:
            stacked(k, onehot)
            scatter(k, 0, na - 1)

    mine = owncol[pl.ds(pl.multiple_of(me * OWN, OWN), OWN), :]
    for c in range(size // LANES):
        lane = lax.broadcasted_iota(jnp.int32, (OWN, LANES), 1) + c * LANES
        mask[:, c * LANES : (c + 1) * LANES] = jnp.where(lane >= mine, 1.0, 0.0)

    load_lat.wait()
    load_cot.wait()
    load_step.wait()
    for c in range(2):
        for s in range(2):
            g = 2 * c + s
            coef[g * OWN : (g + 1) * OWN, :] = jnp.where(
                mask[...] > 0.0, cot_ref[c, s].astype(F32), 0.0
            ).astype(BF16)
    stacked(4, lat)

    load_wave.wait()
    part = min(512, points)
    wide_steps = points // part
    tall_steps = size // tall

    def permute(i, carry):
        s = i // (wide_steps * tall_steps)
        rest = lax.rem(i, wide_steps * tall_steps)
        columns = pl.ds(pl.multiple_of(lax.rem(rest, wide_steps) * part, part), part)
        top = pl.multiple_of((rest // wide_steps) * tall, tall)
        table[s, pl.ds(top, tall), columns] = dot(
            onehot[pl.ds(top, tall), :], nat[s, :, columns], NN
        ).astype(BF16)
        return carry

    lax.fori_loop(0, 2 * wide_steps * tall_steps, permute, 0)

    arrived(0)

    def keep_toroidal(g, columns, tile):
        listed[2 * (g // 2), g % 2, :, columns] = tile.astype(BF16)
        coef[g * OWN : (g + 1) * OWN, columns] = jnp.where(
            mask[:, columns] > 0.0, tile, 0.0
        ).astype(BF16)

    regroup(0, keep_toroidal)
    stacked(2, lat)
    scatter(2, 0, na - 1)

    early, late = na // 4 + 1, na // 2 + 1
    scatter(4, early, late)

    arrived(1)

    def keep_poloidal(g, columns, tile):
        listed[2 * (g // 2) + 1, g % 2, :, columns] = tile.astype(BF16)
        rows[g * OWN : (g + 1) * OWN, columns] = tile.astype(BF16)

    regroup(1, keep_poloidal)
    halo_start(rows, fwd_halo, 0)
    halo_wait(rows, fwd_halo, 0)
    for g in range(4):
        at = slice(g * OWN, (g + 1) * OWN)
        slope = 0.5 * (fwd_halo[1, at, :].astype(F32) - fwd_halo[0, at, :].astype(F32))
        coef[at, :] = jnp.where(mask[...] > 0.0, slope, 0.0).astype(BF16)
    stacked(3, lat)
    scatter(3, 0, na - 1)
    scatter(4, 0, early)
    scatter(4, late, na - 1)

    def into_grid(base):
        def put(g, columns, tile):
            grid[base + g // 2, g % 2, :, columns] = tile.astype(BF16)

        return put

    arrived(2)
    regroup(2, into_grid(0))
    arrived(3)
    regroup(3, into_grid(2))

    def on_grid(first, count, columns):
        left = grid[first : first + count]
        total = None
        for s in range(2):
            part = dot(
                left[:, s].reshape(count * OWN, size), table[s, :, columns], NN
            )
            total = part if total is None else total + part
        total = total * scale
        return [total[c * OWN : (c + 1) * OWN] for c in range(count)]

    def terms(i, carry):
        columns = pl.ds(pl.multiple_of(i * wide, wide), wide)
        vel_tor, mag_tor, vel_pol, mag_pol = on_grid(0, 4, columns)
        for c, value in enumerate((vel_tor, mag_tor, vel_pol, mag_pol)):
            field[c, :, columns] = value
        back_send[0:OWN, columns] = (mag_tor * mag_pol - vel_tor * vel_pol).astype(BF16)
        back_send[OWN : 2 * OWN, columns] = (vel_tor * mag_pol - vel_pol * mag_tor).astype(BF16)
        return carry

    def analyse(k, source):
        def analysed(at):
            parts = [dot(table[s, at, :], source[...], NT) for s in range(2)]
            return scale * jnp.concatenate(parts, axis=1)

        made(k, tall, analysed)
        scatter(k, 0, na - 1)

    lax.fori_loop(0, points // wide, terms, 0)
    analyse(5, back_send)

    arrived(4)
    regroup(4, into_grid(4))
    tor_grad = back_halo.at[2]

    def grads(i, carry):
        columns = pl.ds(pl.multiple_of(i * wide, wide), wide)
        adj_vel, adj_mag = on_grid(4, 2, columns)
        vel_tor, mag_tor, vel_pol, mag_pol = (field[c, :, columns] for c in range(4))
        back_send[0:OWN, columns] = (-vel_tor * adj_vel - mag_tor * adj_mag).astype(BF16)
        back_send[OWN : 2 * OWN, columns] = (mag_tor * adj_vel + vel_tor * adj_mag).astype(BF16)
        tor_grad[0:OWN, columns] = (-vel_pol * adj_vel + mag_pol * adj_mag).astype(BF16)
        tor_grad[OWN : 2 * OWN, columns] = (mag_pol * adj_vel - vel_pol * adj_mag).astype(BF16)
        return carry

    lax.fori_loop(0, points // wide, grads, 0)
    halo_start(back_send, back_halo, 2)
    analyse(6, tor_grad)
    halo_wait(back_send, back_halo, 2)
    tor_grad[...] = (
        0.5 * (back_halo[0].astype(F32) - back_halo[1].astype(F32))
    ).astype(BF16)
    analyse(7, tor_grad)

    step = jnp.broadcast_to(step_ref[...].reshape(1, 1), (OWN, size))

    def finish(k, put):
        arrived(k)

        def keep(g, columns, tile):
            rows[g * OWN : (g + 1) * OWN, columns] = tile.astype(BF16)

        if k == 5:
            halo_sent(rows, fwd_halo, 0)
        regroup(k, keep)

        result = dot(rows[...], lat[...], NN)
        live = mask[...] > 0.0
        for g in range(4):
            put(g // 2, g % 2, jnp.where(live, result[g * OWN : (g + 1) * OWN], 0.0))

    def put_term(s, c, value):
        non_ref[c, s] = value

    def put_seed(first):
        def put(s, c, value):
            channel = 2 * c + first
            next_ref[channel, s] = listed[channel, s].astype(F32) - step * value

        return put

    finish(5, put_term)
    finish(6, put_seed(0))
    finish(7, put_seed(1))
    halo_sent(back_send, back_halo, 2)
    for k in range(8):
        sent(k)


def settle(non_in, next_in, non_out, next_out, store_sem):
    stores = []
    for src, dst in ((next_in, next_out), (non_in, non_out)):
        for c in range(src.shape[0]):
            for s in range(2):
                stores.append(
                    pltpu.make_async_copy(src.at[c, s], dst.at[c, s], store_sem.at[len(stores)])
                )
    for store in stores:
        store.start()
    for store in stores:
        store.wait()


def local(lat_table, wave_table, seed_field, cotangent, step_size, owner_list):
    na = lax.axis_size("ma")
    nr = lax.axis_size("row")
    size = na * OWN
    points = 2 * size
    hbm = pl.BlockSpec(memory_space=pl.ANY)
    shapes = (
        jax.ShapeDtypeStruct((2, 2, OWN, size), F32),
        jax.ShapeDtypeStruct((4, 2, OWN, size), F32),
    )
    outputs = pl.pallas_call(
        functools.partial(kernel, na, nr),
        out_shape=(pltpu.VMEM(shapes[0].shape, F32), pltpu.VMEM(shapes[1].shape, F32)),
        in_specs=[pl.BlockSpec(memory_space=pltpu.HBM)] * 6,
        out_specs=(pl.BlockSpec(memory_space=pltpu.VMEM),) * 2,
        scratch_shapes=[
            pltpu.VMEM((4, 2, OWN, size), BF16),
            pltpu.VMEM((2, 2, OWN, size), BF16),
            pltpu.VMEM((1,), F32),
            pltpu.VMEM((1, size), jnp.int32),
            pltpu.VMEM((size, size), BF16),
            pltpu.VMEM((2, size, points), BF16),
            pltpu.VMEM((2, size, points), BF16),
            pltpu.VMEM((size, size), BF16),
            pltpu.VMEM((size, LANES), jnp.int32),
            pltpu.VMEM((OWN, size), F32),
            pltpu.VMEM((4 * OWN, size), BF16),
            pltpu.VMEM((4, 2, OWN, size), BF16),
            pltpu.VMEM((4 * OWN, size), BF16),
            pltpu.VMEM((6, 2, OWN, size), BF16),
            pltpu.VMEM((4, OWN, points), F32),
            pltpu.VMEM((2, 4 * OWN, size), BF16),
            pltpu.VMEM((2 * OWN, points), BF16),
            pltpu.VMEM((3, 2 * OWN, points), BF16),
            pltpu.VMEM((8, size, LANES), BF16),
            pltpu.VMEM((8, na, OWN, LANES), BF16),
            pltpu.SemaphoreType.DMA((6,)),
            pltpu.SemaphoreType.DMA((8,)),
            pltpu.SemaphoreType.DMA((8,)),
            pltpu.SemaphoreType.DMA((4,)),
            pltpu.SemaphoreType.DMA((4,)),
        ],
        compiler_params=pltpu.CompilerParams(
            collective_id=0, has_side_effects=True, vmem_limit_bytes=56 << 20
        ),
    )(
        seed_field.reshape(4, 2, OWN, size),
        cotangent.reshape(2, 2, OWN, size),
        step_size,
        owner_list.reshape(1, size),
        lat_table,
        wave_table,
    )
    nonlinear, seed_next = pl.pallas_call(
        settle,
        out_shape=shapes,
        in_specs=[hbm] * 2,
        out_specs=(hbm, hbm),
        scratch_shapes=[
            pltpu.SemaphoreType.DMA((12,)),
        ],
        compiler_params=pltpu.CompilerParams(vmem_limit_bytes=40 << 20),
    )(*outputs)
    return (
        nonlinear.reshape(2, 1, 2, OWN, size),
        seed_next.reshape(4, 1, 2, OWN, size),
    )


def solution(mesh):
    split = P(None, "row", None, "ma", None)
    size = mesh.shape["ma"] * OWN
    lat_table = lat_constant(size)
    wave_table = wave_constant(size, 2 * size)
    body = jax.shard_map(
        local,
        mesh=mesh,
        in_specs=(P(), P(), split, split, P(), P()),
        out_specs=(split, split),
        check_vma=False,
    )

    def run(seed_field, cotangent, step_size, owner_list):
        return body(
            jnp.asarray(lat_table), jnp.asarray(wave_table), seed_field, cotangent, step_size, owner_list
        )

    return run
```

```python
import functools
import math

import jax
import jax.numpy as jnp
import numpy as np
from jax import lax
from jax.experimental import pallas as pl
from jax.experimental.pallas import tpu as pltpu
from jax.sharding import PartitionSpec as P

MESH = pl.DeviceIdType.MESH
LANES = 128
OWN = 32
F32 = jnp.float32
BF16 = jnp.bfloat16

NT = (((1,), (1,)), ((), ()))
NN = (((1,), (0,)), ((), ()))


def lat_constant(size):
    phase = (2 * np.arange(size)[:, None] + 1) * np.arange(size)[None, :] % (4 * size)
    return np.cos(phase * (math.pi / (2 * size))).astype(jnp.bfloat16)


def wave_constant(waves, points):
    phase = np.arange(waves)[:, None] * np.arange(points)[None, :] % points
    angles = phase * (2.0 * math.pi / points)
    return np.stack([np.cos(angles), -np.sin(angles)]).astype(jnp.bfloat16)


def dot(a, b, dims):
    return lax.dot_general(a, b, dims, preferred_element_type=F32)


def kernel(
    na,
    nr,
    seed_hbm,
    cot_hbm,
    step_hbm,
    owner_hbm,
    lat_hbm,
    wave_hbm,
    non_ref,
    next_ref,
    seed_ref,
    cot_ref,
    step_ref,
    owner_ref,
    lat,
    nat,
    table,
    onehot,
    owncol,
    mask,
    coef,
    listed,
    rows,
    grid,
    field,
    fwd_halo,
    back_send,
    back_halo,
    send,
    recv,
    load_sem,
    send_sem,
    recv_sem,
    halo_send_sem,
    halo_recv_sem,
):
    me = lax.axis_index("ma")
    radius = lax.axis_index("row")
    size = na * OWN
    points = 2 * size
    quads = na // 4
    chunk = min(256, size)
    tall = min(512, size)
    wide = min(1024, points)
    scale = 2.0 / size

    has_low = radius > 0
    has_high = radius < nr - 1
    barrier = pltpu.get_barrier_semaphore()

    loads = [
        pltpu.make_async_copy(src, dst, load_sem.at[i])
        for i, (src, dst) in enumerate(
            (
                (owner_hbm, owner_ref),
                (seed_hbm, seed_ref),
                (lat_hbm, lat),
                (cot_hbm, cot_ref),
                (step_hbm, step_ref),
                (wave_hbm, nat),
            )
        )
    ]
    load_owner, load_seed, load_lat, load_cot, load_step, load_wave = loads
    load_owner.start()
    load_seed.start()

    def farthest(i):
        return lax.rem(me + na // 2 + (i + 1) // 2 * (1 - 2 * lax.rem(i, 2)), na)

    def greet(i, carry):
        pl.semaphore_signal(barrier, inc=1, device_id={"ma": farthest(i)}, device_id_type=MESH)
        return carry

    lax.fori_loop(0, na - 1, greet, 0)

    @pl.when(has_low)
    def _():
        pl.semaphore_signal(barrier, inc=1, device_id={"row": radius - 1}, device_id_type=MESH)

    @pl.when(has_high)
    def _():
        pl.semaphore_signal(barrier, inc=1, device_id={"row": radius + 1}, device_id_type=MESH)

    for load in loads[2:]:
        load.start()

    def send_block(k, peer):
        pltpu.make_async_remote_copy(
            src_ref=send.at[k, pl.ds(pl.multiple_of(peer * OWN, OWN), OWN), :],
            dst_ref=recv.at[k, me],
            send_sem=send_sem.at[k],
            recv_sem=recv_sem.at[k],
            device_id={"ma": peer},
            device_id_type=MESH,
        ).start()

    def keep_own(k):
        recv[k, me] = send[k, pl.ds(pl.multiple_of(me * OWN, OWN), OWN), :]

    def scatter(k, first, last):
        def one(i, carry):
            send_block(k, farthest(i))
            return carry

        lax.fori_loop(first, last, one, 0)

    def made(k, height, rows_of):
        def one(i, carry):
            at = pl.ds(pl.multiple_of(i * height, height), height)
            send[k, at, :] = rows_of(at).astype(BF16)
            return carry

        lax.fori_loop(0, size // height, one, 0)
        keep_own(k)

    def made_in_turn(k, height, rows_of):
        count = size // height
        peers = height // OWN

        def one(i, carry):
            turn = lax.rem(me // peers + count // 2 + i + i * (i - 1) // 2, count)
            at = pl.ds(pl.multiple_of(turn * height, height), height)
            send[k, at, :] = rows_of(at).astype(BF16)

            def block(j, carry):
                peer = turn * peers + j

                @pl.when(peer != me)
                def _():
                    send_block(k, peer)

                return carry

            lax.fori_loop(0, peers, block, 0)
            return carry

        lax.fori_loop(0, count, one, 0)
        keep_own(k)

    def arrived(k):
        part = recv.at[k, pl.ds(0, na - 1)]
        pltpu.make_async_copy(part, part, recv_sem.at[k]).wait()

    def sent(k):
        part = send.at[k, pl.ds(0, (na - 1) * OWN), :]
        pltpu.make_async_copy(part, part, send_sem.at[k]).wait()

    def halo_copies(src, dst, base):
        down = pltpu.make_async_remote_copy(
            src_ref=src,
            dst_ref=dst.at[1],
            send_sem=halo_send_sem.at[base],
            recv_sem=halo_recv_sem.at[base + 1],
            device_id={"row": jnp.maximum(radius - 1, 0)},
            device_id_type=MESH,
        )
        up = pltpu.make_async_remote_copy(
            src_ref=src,
            dst_ref=dst.at[0],
            send_sem=halo_send_sem.at[base + 1],
            recv_sem=halo_recv_sem.at[base],
            device_id={"row": jnp.minimum(radius + 1, nr - 1)},
            device_id_type=MESH,
        )
        return down, up

    def halo_start(src, dst, base):
        height = src.shape[0] // 4

        def piece(i, carry):
            at = pl.ds(pl.multiple_of(i * height, height), height)
            down, up = halo_copies(src.at[at], dst.at[:, at], base)

            @pl.when(has_low)
            def _():
                down.start()

            @pl.when(has_high)
            def _():
                up.start()

            return carry

        lax.fori_loop(0, 4, piece, 0)

        @pl.when(jnp.logical_not(has_low))
        def _():
            dst[0] = jnp.zeros_like(dst[0])

        @pl.when(jnp.logical_not(has_high))
        def _():
            dst[1] = jnp.zeros_like(dst[1])

    def halo_wait(src, dst, base):
        down, up = halo_copies(src, dst, base)

        @pl.when(has_low)
        def _():
            up.wait_recv()

        @pl.when(has_high)
        def _():
            down.wait_recv()

    def halo_sent(src, dst, base):
        down, up = halo_copies(src, dst, base)

        @pl.when(has_low)
        def _():
            down.wait_send()

        @pl.when(has_high)
        def _():
            up.wait_send()

    group = lax.broadcasted_iota(jnp.int32, (OWN, LANES), 1) // OWN
    odd = lax.rem(group, 2) == 1
    high = group >= 2

    def regroup(k, put):
        def one(q, carry):
            x = [recv[k, 4 * q + a].astype(F32) for a in range(4)]
            y = [None] * 4
            for a in (0, 2):
                y[a] = jnp.where(odd, pltpu.roll(x[a + 1], 32, 1), x[a])
                y[a + 1] = jnp.where(odd, x[a + 1], pltpu.roll(x[a], 96, 1))
            z = [None] * 4
            for a in (0, 1):
                z[a] = jnp.where(high, pltpu.roll(y[a + 2], 64, 1), y[a])
                z[a + 2] = jnp.where(high, y[a + 2], pltpu.roll(y[a], 64, 1))
            columns = pl.ds(pl.multiple_of(q * LANES, LANES), LANES)
            for g in range(4):
                put(g, columns, z[g])
            return carry

        lax.fori_loop(0, quads, one, 0, unroll=min(4, quads))

    def stacked(k, left):
        made(k, tall, lambda at: dot(left[at, :], coef[...], NT))

    def order(at):
        for b in range(at.size // LANES):
            block = pl.ds(pl.multiple_of(at.start + b * LANES, LANES), LANES)
            column = jnp.transpose(jnp.broadcast_to(owner_ref[0:1, block], (LANES, LANES)))
            owncol[block, :] = column
            lane = lax.broadcasted_iota(jnp.int32, (LANES, LANES), 1)
            for c in range(size // LANES):
                onehot[block, c * LANES : (c + 1) * LANES] = jnp.where(
                    column == lane + c * LANES, 1.0, 0.0
                ).astype(BF16)

    def ordered(at):
        order(at)
        return dot(onehot[at, :], coef[...], NT)

    load_seed.wait()
    load_owner.wait()
    for k in range(2):
        for c in range(2):
            for s in range(2):
                g = 2 * c + s
                coef[g * OWN : (g + 1) * OWN, :] = seed_ref[k + 2 * c, s]
        if k == 0:
            made(k, chunk, ordered)
            pl.semaphore_wait(
                barrier, na - 1 + has_low.astype(jnp.int32) + has_high.astype(jnp.int32)
            )
        else:
            stacked(k, onehot)
        scatter(k, 0, na - 1)

    mine = owncol[pl.ds(pl.multiple_of(me * OWN, OWN), OWN), :]
    for c in range(size // LANES):
        lane = lax.broadcasted_iota(jnp.int32, (OWN, LANES), 1) + c * LANES
        mask[:, c * LANES : (c + 1) * LANES] = jnp.where(lane >= mine, 1.0, 0.0)

    load_lat.wait()
    load_cot.wait()
    load_step.wait()
    for c in range(2):
        for s in range(2):
            g = 2 * c + s
            coef[g * OWN : (g + 1) * OWN, :] = jnp.where(
                mask[...] > 0.0, cot_ref[c, s].astype(F32), 0.0
            ).astype(BF16)
    stacked(4, lat)

    load_wave.wait()
    part = min(512, points)
    wide_steps = points // part
    tall_steps = size // tall

    def permute(i, carry):
        s = i // (wide_steps * tall_steps)
        rest = lax.rem(i, wide_steps * tall_steps)
        columns = pl.ds(pl.multiple_of(lax.rem(rest, wide_steps) * part, part), part)
        top = pl.multiple_of((rest // wide_steps) * tall, tall)
        table[s, pl.ds(top, tall), columns] = dot(
            onehot[pl.ds(top, tall), :], nat[s, :, columns], NN
        ).astype(BF16)
        return carry

    lax.fori_loop(0, 2 * wide_steps * tall_steps, permute, 0)

    arrived(0)

    def keep_toroidal(g, columns, tile):
        listed[2 * (g // 2), g % 2, :, columns] = tile.astype(BF16)
        coef[g * OWN : (g + 1) * OWN, columns] = jnp.where(
            mask[:, columns] > 0.0, tile, 0.0
        ).astype(BF16)

    regroup(0, keep_toroidal)
    made_in_turn(2, chunk, lambda at: dot(lat[at, :], coef[...], NT))

    early, late = na // 4 + 1, na // 2 + 1
    scatter(4, early, late)

    arrived(1)

    def keep_poloidal(g, columns, tile):
        listed[2 * (g // 2) + 1, g % 2, :, columns] = tile.astype(BF16)
        rows[g * OWN : (g + 1) * OWN, columns] = tile.astype(BF16)

    regroup(1, keep_poloidal)
    halo_start(rows, fwd_halo, 0)
    halo_wait(rows, fwd_halo, 0)
    for g in range(4):
        at = slice(g * OWN, (g + 1) * OWN)
        slope = 0.5 * (fwd_halo[1, at, :].astype(F32) - fwd_halo[0, at, :].astype(F32))
        coef[at, :] = jnp.where(mask[...] > 0.0, slope, 0.0).astype(BF16)
    made_in_turn(3, chunk, lambda at: dot(lat[at, :], coef[...], NT))
    scatter(4, 0, early)
    scatter(4, late, na - 1)

    def into_grid(base):
        def put(g, columns, tile):
            grid[base + g // 2, g % 2, :, columns] = tile.astype(BF16)

        return put

    arrived(2)
    regroup(2, into_grid(0))
    arrived(3)
    regroup(3, into_grid(2))

    def on_grid(first, count, columns):
        left = grid[first : first + count]
        total = None
        for s in range(2):
            part = dot(
                left[:, s].reshape(count * OWN, size), table[s, :, columns], NN
            )
            total = part if total is None else total + part
        total = total * scale
        return [total[c * OWN : (c + 1) * OWN] for c in range(count)]

    def terms(i, carry):
        columns = pl.ds(pl.multiple_of(i * wide, wide), wide)
        vel_tor, mag_tor, vel_pol, mag_pol = on_grid(0, 4, columns)
        for c, value in enumerate((vel_tor, mag_tor, vel_pol, mag_pol)):
            field[c, :, columns] = value
        back_send[0:OWN, columns] = (mag_tor * mag_pol - vel_tor * vel_pol).astype(BF16)
        back_send[OWN : 2 * OWN, columns] = (vel_tor * mag_pol - vel_pol * mag_tor).astype(BF16)
        return carry

    def analyse(k, source):
        def analysed(at):
            parts = [dot(table[s, at, :], source[...], NT) for s in range(2)]
            return scale * jnp.concatenate(parts, axis=1)

        made_in_turn(k, tall, analysed)

    lax.fori_loop(0, points // wide, terms, 0)
    analyse(5, back_send)

    arrived(4)
    regroup(4, into_grid(4))
    tor_grad = back_halo.at[2]

    def grads(i, carry):
        columns = pl.ds(pl.multiple_of(i * wide, wide), wide)
        adj_vel, adj_mag = on_grid(4, 2, columns)
        vel_tor, mag_tor, vel_pol, mag_pol = (field[c, :, columns] for c in range(4))
        back_send[0:OWN, columns] = (-vel_tor * adj_vel - mag_tor * adj_mag).astype(BF16)
        back_send[OWN : 2 * OWN, columns] = (mag_tor * adj_vel + vel_tor * adj_mag).astype(BF16)
        tor_grad[0:OWN, columns] = (-vel_pol * adj_vel + mag_pol * adj_mag).astype(BF16)
        tor_grad[OWN : 2 * OWN, columns] = (mag_pol * adj_vel - vel_pol * adj_mag).astype(BF16)
        return carry

    lax.fori_loop(0, points // wide, grads, 0)
    halo_start(back_send, back_halo, 2)
    analyse(6, tor_grad)
    halo_wait(back_send, back_halo, 2)
    tor_grad[...] = (
        0.5 * (back_halo[0].astype(F32) - back_halo[1].astype(F32))
    ).astype(BF16)
    analyse(7, tor_grad)

    step = jnp.broadcast_to(step_ref[...].reshape(1, 1), (OWN, size))

    def finish(k, put):
        arrived(k)

        def keep(g, columns, tile):
            rows[g * OWN : (g + 1) * OWN, columns] = tile.astype(BF16)

        if k == 5:
            halo_sent(rows, fwd_halo, 0)
        regroup(k, keep)

        result = dot(rows[...], lat[...], NN)
        live = mask[...] > 0.0
        for g in range(4):
            put(g // 2, g % 2, jnp.where(live, result[g * OWN : (g + 1) * OWN], 0.0))

    def put_term(s, c, value):
        non_ref[c, s] = value

    def put_seed(first):
        def put(s, c, value):
            channel = 2 * c + first
            next_ref[channel, s] = listed[channel, s].astype(F32) - step * value

        return put

    finish(5, put_term)
    finish(6, put_seed(0))
    finish(7, put_seed(1))
    halo_sent(back_send, back_halo, 2)
    for k in range(8):
        sent(k)


def settle(non_in, next_in, non_out, next_out, store_sem):
    stores = []
    for src, dst in ((next_in, next_out), (non_in, non_out)):
        for c in range(src.shape[0]):
            for s in range(2):
                stores.append(
                    pltpu.make_async_copy(src.at[c, s], dst.at[c, s], store_sem.at[len(stores)])
                )
    for store in stores:
        store.start()
    for store in stores:
        store.wait()


def local(lat_table, wave_table, seed_field, cotangent, step_size, owner_list):
    na = lax.axis_size("ma")
    nr = lax.axis_size("row")
    size = na * OWN
    points = 2 * size
    hbm = pl.BlockSpec(memory_space=pl.ANY)
    shapes = (
        jax.ShapeDtypeStruct((2, 2, OWN, size), F32),
        jax.ShapeDtypeStruct((4, 2, OWN, size), F32),
    )
    outputs = pl.pallas_call(
        functools.partial(kernel, na, nr),
        out_shape=(pltpu.VMEM(shapes[0].shape, F32), pltpu.VMEM(shapes[1].shape, F32)),
        in_specs=[pl.BlockSpec(memory_space=pltpu.HBM)] * 6,
        out_specs=(pl.BlockSpec(memory_space=pltpu.VMEM),) * 2,
        scratch_shapes=[
            pltpu.VMEM((4, 2, OWN, size), BF16),
            pltpu.VMEM((2, 2, OWN, size), BF16),
            pltpu.VMEM((1,), F32),
            pltpu.VMEM((1, size), jnp.int32),
            pltpu.VMEM((size, size), BF16),
            pltpu.VMEM((2, size, points), BF16),
            pltpu.VMEM((2, size, points), BF16),
            pltpu.VMEM((size, size), BF16),
            pltpu.VMEM((size, LANES), jnp.int32),
            pltpu.VMEM((OWN, size), F32),
            pltpu.VMEM((4 * OWN, size), BF16),
            pltpu.VMEM((4, 2, OWN, size), BF16),
            pltpu.VMEM((4 * OWN, size), BF16),
            pltpu.VMEM((6, 2, OWN, size), BF16),
            pltpu.VMEM((4, OWN, points), F32),
            pltpu.VMEM((2, 4 * OWN, size), BF16),
            pltpu.VMEM((2 * OWN, points), BF16),
            pltpu.VMEM((3, 2 * OWN, points), BF16),
            pltpu.VMEM((8, size, LANES), BF16),
            pltpu.VMEM((8, na, OWN, LANES), BF16),
            pltpu.SemaphoreType.DMA((6,)),
            pltpu.SemaphoreType.DMA((8,)),
            pltpu.SemaphoreType.DMA((8,)),
            pltpu.SemaphoreType.DMA((4,)),
            pltpu.SemaphoreType.DMA((4,)),
        ],
        compiler_params=pltpu.CompilerParams(
            collective_id=0, has_side_effects=True, vmem_limit_bytes=56 << 20
        ),
    )(
        seed_field.reshape(4, 2, OWN, size),
        cotangent.reshape(2, 2, OWN, size),
        step_size,
        owner_list.reshape(1, size),
        lat_table,
        wave_table,
    )
    nonlinear, seed_next = pl.pallas_call(
        settle,
        out_shape=shapes,
        in_specs=[hbm] * 2,
        out_specs=(hbm, hbm),
        scratch_shapes=[
            pltpu.SemaphoreType.DMA((12,)),
        ],
        compiler_params=pltpu.CompilerParams(vmem_limit_bytes=40 << 20),
    )(*outputs)
    return (
        nonlinear.reshape(2, 1, 2, OWN, size),
        seed_next.reshape(4, 1, 2, OWN, size),
    )


def solution(mesh):
    split = P(None, "row", None, "ma", None)
    size = mesh.shape["ma"] * OWN
    lat_table = lat_constant(size)
    wave_table = wave_constant(size, 2 * size)
    body = jax.shard_map(
        local,
        mesh=mesh,
        in_specs=(P(), P(), split, split, P(), P()),
        out_specs=(split, split),
        check_vma=False,
    )

    def run(seed_field, cotangent, step_size, owner_list):
        return body(
            jnp.asarray(lat_table), jnp.asarray(wave_table), seed_field, cotangent, step_size, owner_list
        )

    return run
```

```python
import functools
import math

import jax
import jax.numpy as jnp
import numpy as np
from jax import lax
from jax.experimental import pallas as pl
from jax.experimental.pallas import tpu as pltpu
from jax.sharding import PartitionSpec as P

MESH = pl.DeviceIdType.MESH
LANES = 128
OWN = 32
F32 = jnp.float32
BF16 = jnp.bfloat16

NT = (((1,), (1,)), ((), ()))
NN = (((1,), (0,)), ((), ()))


def lat_constant(size):
    phase = (2 * np.arange(size)[:, None] + 1) * np.arange(size)[None, :] % (4 * size)
    return np.cos(phase * (math.pi / (2 * size))).astype(jnp.bfloat16)


def wave_constant(waves, points):
    phase = np.arange(waves)[:, None] * np.arange(points)[None, :] % points
    angles = phase * (2.0 * math.pi / points)
    return np.stack([np.cos(angles), -np.sin(angles)]).astype(jnp.bfloat16)


def dot(a, b, dims):
    return lax.dot_general(a, b, dims, preferred_element_type=F32)


def kernel(
    na,
    nr,
    seed_hbm,
    cot_hbm,
    step_hbm,
    owner_hbm,
    lat_hbm,
    wave_hbm,
    non_ref,
    next_ref,
    seed_ref,
    cot_ref,
    step_ref,
    owner_ref,
    lat,
    nat,
    table,
    onehot,
    owncol,
    mask,
    coef,
    listed,
    rows,
    spec,
    grid,
    field,
    fwd_halo,
    back_send,
    back_halo,
    send,
    recv,
    load_sem,
    send_sem,
    recv_sem,
    halo_send_sem,
    halo_recv_sem,
):
    me = lax.axis_index("ma")
    radius = lax.axis_index("row")
    size = na * OWN
    points = 2 * size
    quads = na // 4
    chunk = min(256, size)
    tall = min(512, size)
    wide = min(1024, points)
    scale = 2.0 / size

    has_low = radius > 0
    has_high = radius < nr - 1
    barrier = pltpu.get_barrier_semaphore()

    loads = [
        pltpu.make_async_copy(src, dst, load_sem.at[i])
        for i, (src, dst) in enumerate(
            (
                (owner_hbm, owner_ref),
                (seed_hbm, seed_ref),
                (lat_hbm, lat),
                (cot_hbm, cot_ref),
                (step_hbm, step_ref),
                (wave_hbm, nat),
            )
        )
    ]
    load_owner, load_seed, load_lat, load_cot, load_step, load_wave = loads
    load_owner.start()
    load_seed.start()

    def farthest(i):
        return lax.rem(me + na // 2 + (i + 1) // 2 * (1 - 2 * lax.rem(i, 2)), na)

    def greet(i, carry):
        pl.semaphore_signal(barrier, inc=1, device_id={"ma": farthest(i)}, device_id_type=MESH)
        return carry

    lax.fori_loop(0, na - 1, greet, 0)

    @pl.when(has_low)
    def _():
        pl.semaphore_signal(barrier, inc=1, device_id={"row": radius - 1}, device_id_type=MESH)

    @pl.when(has_high)
    def _():
        pl.semaphore_signal(barrier, inc=1, device_id={"row": radius + 1}, device_id_type=MESH)

    for load in loads[2:]:
        load.start()

    def send_block(k, peer):
        pltpu.make_async_remote_copy(
            src_ref=send.at[k, pl.ds(pl.multiple_of(peer * OWN, OWN), OWN), :],
            dst_ref=recv.at[k, me],
            send_sem=send_sem.at[k],
            recv_sem=recv_sem.at[k],
            device_id={"ma": peer},
            device_id_type=MESH,
        ).start()

    def keep_own(k):
        recv[k, me] = send[k, pl.ds(pl.multiple_of(me * OWN, OWN), OWN), :]

    def scatter(k, first, last):
        def one(i, carry):
            send_block(k, farthest(i))
            return carry

        lax.fori_loop(first, last, one, 0)

    def made(k, height, rows_of):
        def one(i, carry):
            at = pl.ds(pl.multiple_of(i * height, height), height)
            send[k, at, :] = rows_of(at).astype(BF16)
            return carry

        lax.fori_loop(0, size // height, one, 0)
        keep_own(k)

    def made_in_turn(k, height, rows_of):
        count = size // height
        peers = height // OWN

        def one(i, carry):
            turn = lax.rem(me // peers + count // 2 + i + i * (i - 1) // 2, count)
            at = pl.ds(pl.multiple_of(turn * height, height), height)
            send[k, at, :] = rows_of(at).astype(BF16)

            def block(j, carry):
                peer = turn * peers + j

                @pl.when(peer != me)
                def _():
                    send_block(k, peer)

                return carry

            lax.fori_loop(0, peers, block, 0)
            return carry

        lax.fori_loop(0, count, one, 0)
        keep_own(k)

    def arrived(k):
        part = recv.at[k, pl.ds(0, na - 1)]
        pltpu.make_async_copy(part, part, recv_sem.at[k]).wait()

    def sent(k):
        part = send.at[k, pl.ds(0, (na - 1) * OWN), :]
        pltpu.make_async_copy(part, part, send_sem.at[k]).wait()

    def halo_copies(src, dst, base):
        down = pltpu.make_async_remote_copy(
            src_ref=src,
            dst_ref=dst.at[1],
            send_sem=halo_send_sem.at[base],
            recv_sem=halo_recv_sem.at[base + 1],
            device_id={"row": jnp.maximum(radius - 1, 0)},
            device_id_type=MESH,
        )
        up = pltpu.make_async_remote_copy(
            src_ref=src,
            dst_ref=dst.at[0],
            send_sem=halo_send_sem.at[base + 1],
            recv_sem=halo_recv_sem.at[base],
            device_id={"row": jnp.minimum(radius + 1, nr - 1)},
            device_id_type=MESH,
        )
        return down, up

    def halo_start(src, dst, base):
        height = src.shape[0] // 4

        def piece(i, carry):
            at = pl.ds(pl.multiple_of(i * height, height), height)
            down, up = halo_copies(src.at[at], dst.at[:, at], base)

            @pl.when(has_low)
            def _():
                down.start()

            @pl.when(has_high)
            def _():
                up.start()

            return carry

        lax.fori_loop(0, 4, piece, 0)

        @pl.when(jnp.logical_not(has_low))
        def _():
            dst[0] = jnp.zeros_like(dst[0])

        @pl.when(jnp.logical_not(has_high))
        def _():
            dst[1] = jnp.zeros_like(dst[1])

    def halo_wait(src, dst, base):
        down, up = halo_copies(src, dst, base)

        @pl.when(has_low)
        def _():
            up.wait_recv()

        @pl.when(has_high)
        def _():
            down.wait_recv()

    def halo_sent(src, dst, base):
        down, up = halo_copies(src, dst, base)

        @pl.when(has_low)
        def _():
            down.wait_send()

        @pl.when(has_high)
        def _():
            up.wait_send()

    group = lax.broadcasted_iota(jnp.int32, (OWN, LANES), 1) // OWN
    odd = lax.rem(group, 2) == 1
    high = group >= 2

    def regroup(k, put):
        def one(q, carry):
            x = [recv[k, 4 * q + a].astype(F32) for a in range(4)]
            y = [None] * 4
            for a in (0, 2):
                y[a] = jnp.where(odd, pltpu.roll(x[a + 1], 32, 1), x[a])
                y[a + 1] = jnp.where(odd, x[a + 1], pltpu.roll(x[a], 96, 1))
            z = [None] * 4
            for a in (0, 1):
                z[a] = jnp.where(high, pltpu.roll(y[a + 2], 64, 1), y[a])
                z[a + 2] = jnp.where(high, y[a + 2], pltpu.roll(y[a], 64, 1))
            columns = pl.ds(pl.multiple_of(q * LANES, LANES), LANES)
            for g in range(4):
                put(g, columns, z[g])
            return carry

        lax.fori_loop(0, quads, one, 0, unroll=min(4, quads))

    def stacked(k, left):
        made(k, tall, lambda at: dot(left[at, :], coef[...], NT))

    def order(at):
        for b in range(at.size // LANES):
            block = pl.ds(pl.multiple_of(at.start + b * LANES, LANES), LANES)
            column = jnp.transpose(jnp.broadcast_to(owner_ref[0:1, block], (LANES, LANES)))
            owncol[block, :] = column
            lane = lax.broadcasted_iota(jnp.int32, (LANES, LANES), 1)
            for c in range(size // LANES):
                onehot[block, c * LANES : (c + 1) * LANES] = jnp.where(
                    column == lane + c * LANES, 1.0, 0.0
                ).astype(BF16)

    def ordered(at):
        order(at)
        return dot(onehot[at, :], coef[...], NT)

    load_seed.wait()
    load_owner.wait()
    for k in range(2):
        for c in range(2):
            for s in range(2):
                g = 2 * c + s
                coef[g * OWN : (g + 1) * OWN, :] = seed_ref[k + 2 * c, s]
        if k == 0:
            made(k, chunk, ordered)
            pl.semaphore_wait(
                barrier, na - 1 + has_low.astype(jnp.int32) + has_high.astype(jnp.int32)
            )
        else:
            stacked(k, onehot)
        scatter(k, 0, na - 1)

    mine = owncol[pl.ds(pl.multiple_of(me * OWN, OWN), OWN), :]
    for c in range(size // LANES):
        lane = lax.broadcasted_iota(jnp.int32, (OWN, LANES), 1) + c * LANES
        mask[:, c * LANES : (c + 1) * LANES] = jnp.where(lane >= mine, 1.0, 0.0)

    load_lat.wait()
    load_cot.wait()
    load_step.wait()
    for c in range(2):
        for s in range(2):
            g = 2 * c + s
            coef[g * OWN : (g + 1) * OWN, :] = jnp.where(
                mask[...] > 0.0, cot_ref[c, s].astype(F32), 0.0
            ).astype(BF16)
    stacked(4, lat)

    load_wave.wait()
    part = min(512, points)
    wide_steps = points // part
    tall_steps = size // tall

    def permute(i, carry):
        s = i // (wide_steps * tall_steps)
        rest = lax.rem(i, wide_steps * tall_steps)
        columns = pl.ds(pl.multiple_of(lax.rem(rest, wide_steps) * part, part), part)
        top = pl.multiple_of((rest // wide_steps) * tall, tall)
        table[s, pl.ds(top, tall), columns] = dot(
            onehot[pl.ds(top, tall), :], nat[s, :, columns], NN
        ).astype(BF16)
        return carry

    lax.fori_loop(0, 2 * wide_steps * tall_steps, permute, 0)

    arrived(0)

    def keep_toroidal(g, columns, tile):
        listed[2 * (g // 2), g % 2, :, columns] = tile.astype(BF16)
        coef[g * OWN : (g + 1) * OWN, columns] = jnp.where(
            mask[:, columns] > 0.0, tile, 0.0
        ).astype(BF16)

    regroup(0, keep_toroidal)
    made_in_turn(2, chunk, lambda at: dot(lat[at, :], coef[...], NT))

    early, late = na // 4 + 1, na // 2 + 1
    scatter(4, early, late)

    arrived(1)

    def keep_poloidal(g, columns, tile):
        listed[2 * (g // 2) + 1, g % 2, :, columns] = tile.astype(BF16)
        coef[g * OWN : (g + 1) * OWN, columns] = jnp.where(
            mask[:, columns] > 0.0, tile, 0.0
        ).astype(BF16)

    regroup(1, keep_poloidal)

    def poloidal(i, carry):
        at = pl.ds(pl.multiple_of(i * tall, tall), tall)
        spec[at, :] = dot(lat[at, :], coef[...], NT).astype(BF16)
        return carry

    lax.fori_loop(0, size // tall, poloidal, 0)
    halo_start(spec, fwd_halo, 0)
    halo_wait(spec, fwd_halo, 0)
    made_in_turn(
        3,
        chunk,
        lambda at: 0.5 * (fwd_halo[1, at, :].astype(F32) - fwd_halo[0, at, :].astype(F32)),
    )
    scatter(4, 0, early)
    scatter(4, late, na - 1)

    def into_grid(base):
        def put(g, columns, tile):
            grid[base + g // 2, g % 2, :, columns] = tile.astype(BF16)

        return put

    arrived(2)
    regroup(2, into_grid(0))
    arrived(3)
    regroup(3, into_grid(2))

    def on_grid(first, count, columns):
        left = grid[first : first + count]
        total = None
        for s in range(2):
            part = dot(
                left[:, s].reshape(count * OWN, size), table[s, :, columns], NN
            )
            total = part if total is None else total + part
        total = total * scale
        return [total[c * OWN : (c + 1) * OWN] for c in range(count)]

    def terms(i, carry):
        columns = pl.ds(pl.multiple_of(i * wide, wide), wide)
        vel_tor, mag_tor, vel_pol, mag_pol = on_grid(0, 4, columns)
        for c, value in enumerate((vel_tor, mag_tor, vel_pol, mag_pol)):
            field[c, :, columns] = value
        back_send[0:OWN, columns] = (mag_tor * mag_pol - vel_tor * vel_pol).astype(BF16)
        back_send[OWN : 2 * OWN, columns] = (vel_tor * mag_pol - vel_pol * mag_tor).astype(BF16)
        return carry

    def analyse(k, source):
        def analysed(at):
            parts = [dot(table[s, at, :], source[...], NT) for s in range(2)]
            return scale * jnp.concatenate(parts, axis=1)

        made_in_turn(k, tall, analysed)

    lax.fori_loop(0, points // wide, terms, 0)
    analyse(5, back_send)

    arrived(4)
    regroup(4, into_grid(4))
    tor_grad = back_halo.at[2]

    def grads(i, carry):
        columns = pl.ds(pl.multiple_of(i * wide, wide), wide)
        adj_vel, adj_mag = on_grid(4, 2, columns)
        vel_tor, mag_tor, vel_pol, mag_pol = (field[c, :, columns] for c in range(4))
        back_send[0:OWN, columns] = (-vel_tor * adj_vel - mag_tor * adj_mag).astype(BF16)
        back_send[OWN : 2 * OWN, columns] = (mag_tor * adj_vel + vel_tor * adj_mag).astype(BF16)
        tor_grad[0:OWN, columns] = (-vel_pol * adj_vel + mag_pol * adj_mag).astype(BF16)
        tor_grad[OWN : 2 * OWN, columns] = (mag_pol * adj_vel - vel_pol * adj_mag).astype(BF16)
        return carry

    lax.fori_loop(0, points // wide, grads, 0)
    halo_start(back_send, back_halo, 2)
    analyse(6, tor_grad)
    halo_wait(back_send, back_halo, 2)
    tor_grad[...] = (
        0.5 * (back_halo[0].astype(F32) - back_halo[1].astype(F32))
    ).astype(BF16)
    analyse(7, tor_grad)

    step = jnp.broadcast_to(step_ref[...].reshape(1, 1), (OWN, size))

    def finish(k, put):
        arrived(k)

        def keep(g, columns, tile):
            rows[g * OWN : (g + 1) * OWN, columns] = tile.astype(BF16)

        if k == 5:
            halo_sent(spec, fwd_halo, 0)
        regroup(k, keep)

        result = dot(rows[...], lat[...], NN)
        live = mask[...] > 0.0
        for g in range(4):
            put(g // 2, g % 2, jnp.where(live, result[g * OWN : (g + 1) * OWN], 0.0))

    def put_term(s, c, value):
        non_ref[c, s] = value

    def put_seed(first):
        def put(s, c, value):
            channel = 2 * c + first
            next_ref[channel, s] = listed[channel, s].astype(F32) - step * value

        return put

    finish(5, put_term)
    finish(6, put_seed(0))
    finish(7, put_seed(1))
    halo_sent(back_send, back_halo, 2)
    for k in range(8):
        sent(k)


def settle(non_in, next_in, non_out, next_out, store_sem):
    stores = []
    for src, dst in ((next_in, next_out), (non_in, non_out)):
        for c in range(src.shape[0]):
            for s in range(2):
                stores.append(
                    pltpu.make_async_copy(src.at[c, s], dst.at[c, s], store_sem.at[len(stores)])
                )
    for store in stores:
        store.start()
    for store in stores:
        store.wait()


def local(lat_table, wave_table, seed_field, cotangent, step_size, owner_list):
    na = lax.axis_size("ma")
    nr = lax.axis_size("row")
    size = na * OWN
    points = 2 * size
    hbm = pl.BlockSpec(memory_space=pl.ANY)
    shapes = (
        jax.ShapeDtypeStruct((2, 2, OWN, size), F32),
        jax.ShapeDtypeStruct((4, 2, OWN, size), F32),
    )
    outputs = pl.pallas_call(
        functools.partial(kernel, na, nr),
        out_shape=(pltpu.VMEM(shapes[0].shape, F32), pltpu.VMEM(shapes[1].shape, F32)),
        in_specs=[pl.BlockSpec(memory_space=pltpu.HBM)] * 6,
        out_specs=(pl.BlockSpec(memory_space=pltpu.VMEM),) * 2,
        scratch_shapes=[
            pltpu.VMEM((4, 2, OWN, size), BF16),
            pltpu.VMEM((2, 2, OWN, size), BF16),
            pltpu.VMEM((1,), F32),
            pltpu.VMEM((1, size), jnp.int32),
            pltpu.VMEM((size, size), BF16),
            pltpu.VMEM((2, size, points), BF16),
            pltpu.VMEM((2, size, points), BF16),
            pltpu.VMEM((size, size), BF16),
            pltpu.VMEM((size, LANES), jnp.int32),
            pltpu.VMEM((OWN, size), F32),
            pltpu.VMEM((4 * OWN, size), BF16),
            pltpu.VMEM((4, 2, OWN, size), BF16),
            pltpu.VMEM((4 * OWN, size), BF16),
            pltpu.VMEM((size, LANES), BF16),
            pltpu.VMEM((6, 2, OWN, size), BF16),
            pltpu.VMEM((4, OWN, points), F32),
            pltpu.VMEM((2, size, LANES), BF16),
            pltpu.VMEM((2 * OWN, points), BF16),
            pltpu.VMEM((3, 2 * OWN, points), BF16),
            pltpu.VMEM((8, size, LANES), BF16),
            pltpu.VMEM((8, na, OWN, LANES), BF16),
            pltpu.SemaphoreType.DMA((6,)),
            pltpu.SemaphoreType.DMA((8,)),
            pltpu.SemaphoreType.DMA((8,)),
            pltpu.SemaphoreType.DMA((4,)),
            pltpu.SemaphoreType.DMA((4,)),
        ],
        compiler_params=pltpu.CompilerParams(
            collective_id=0, has_side_effects=True, vmem_limit_bytes=56 << 20
        ),
    )(
        seed_field.reshape(4, 2, OWN, size),
        cotangent.reshape(2, 2, OWN, size),
        step_size,
        owner_list.reshape(1, size),
        lat_table,
        wave_table,
    )
    nonlinear, seed_next = pl.pallas_call(
        settle,
        out_shape=shapes,
        in_specs=[hbm] * 2,
        out_specs=(hbm, hbm),
        scratch_shapes=[
            pltpu.SemaphoreType.DMA((12,)),
        ],
        compiler_params=pltpu.CompilerParams(vmem_limit_bytes=40 << 20),
    )(*outputs)
    return (
        nonlinear.reshape(2, 1, 2, OWN, size),
        seed_next.reshape(4, 1, 2, OWN, size),
    )


def solution(mesh):
    split = P(None, "row", None, "ma", None)
    size = mesh.shape["ma"] * OWN
    lat_table = lat_constant(size)
    wave_table = wave_constant(size, 2 * size)
    body = jax.shard_map(
        local,
        mesh=mesh,
        in_specs=(P(), P(), split, split, P(), P()),
        out_specs=(split, split),
        check_vma=False,
    )

    def run(seed_field, cotangent, step_size, owner_list):
        return body(
            jnp.asarray(lat_table), jnp.asarray(wave_table), seed_field, cotangent, step_size, owner_list
        )

    return run
```
